32 devices in a mesh: groups: 2 (over y), tr: 8 (over z, x), tc: 2 (over core).
Axes of the slice: x: 2, y: 2, z: 4, core: 2. Of those that a mesh axis runs over, the one named last changes fastest.
Arguments:
- shift_plane: float32 [2, 8192, 4096], P(None, ('groups', 'tr'), 'tc'), parts along dimension 1, may hold values from -0.2 to 0.2
- height: float32 [8192, 4096], P(('groups', 'tr'), 'tc'), parts along dimension 0, may hold values from -4 to 4
- dipole: float32 [8192, 4096], P(('groups', 'tr'), 'tc'), parts along dimension 0, may hold values from -6 to 6
Outputs:
- velocity_update: float32 [3, 8192, 4096], P(None, ('groups', 'tr'), 'tc'), parts along dimension 1
- dipole_update: float32 [8192, 4096], P(('groups', 'tr'), 'tc'), parts along dimension 0
The draws below stay inside these ranges and needn't reach their ends.
There are 2 independent parts, one for each index of `groups`. The reference program is written for one: setup_inputs(seed, part) draws one part's arguments, and reference() takes and returns one part's arrays. A program takes and returns all parts, laid end to end along the dimension named above; each array names one. Nothing has to cross between parts.
All inputs are finite; a program needn't handle non-finite values.
Results may differ from the reference program's by a relative error of at most 0.00009.
Values sent between devices are 32-bit elements; how exact they have to be, the bound alone decides.
No kernel may reach another device: no remote copies, remote signals or barrier semaphores. Data moves between devices by JAX's collectives and lax.ppermute only.
A program may use at most 256 MiB of HBM per device.

```python
import jax
import jax.numpy as jnp

NB = 4096
NA = 4096


def block_scale(stream_key, dims, pieces, low, top_value):
    def one(position, blocks):
        draws = jax.random.uniform(jax.random.fold_in(jax.random.fold_in(stream_key, 6), position), (blocks,), jnp.float32, low / len(pieces), top_value / len(pieces))
        return jnp.repeat(jnp.exp(draws), dims[position] // blocks).reshape((-1,) + (1,) * (len(dims) - position - 1))

    gain = one(*pieces[0])
    for cut in pieces[1:]:
        gain = gain * one(*cut)
    return gain


def gaussian(rng, dims, width, limit, shards=(), kind=jnp.bfloat16):
    loudness = block_scale(rng, dims, shards, -0.22, 0.18) if shards else 1.0
    array = jax.random.normal(rng, dims, jnp.float32) * width * loudness
    return jnp.minimum(jnp.maximum(array, -limit), limit).astype(kind)


def setup_inputs(seed: int = 0, part: int = 0) -> dict:
    key_list = jax.random.split(jax.random.key(seed), 4)
    part_keys = jax.random.split(jax.random.fold_in(key_list[3], part), 4)
    shift_plane = jnp.clip(jax.random.uniform(part_keys[0], (2, NA, NB), jnp.float32, -0.2, 0.2) * block_scale(part_keys[0], (2, NA, NB), ((1, 8), (2, 2)), -0.4, 0.0), -0.2, 0.2)
    height = gaussian(part_keys[1], (NA, NB), 1.0, 4.0, ((0, 8), (1, 2)), jnp.float32)
    dipole = gaussian(part_keys[2], (NA, NB), 1.0, 6.0, ((0, 8), (1, 2)), jnp.float32)
    return {"shift_plane": shift_plane, "height": height, "dipole": dipole}


def first_diff(field, axis):
    return (jnp.roll(field, 2, axis) - 8.0 * jnp.roll(field, 1, axis) + 8.0 * jnp.roll(field, -1, axis) - jnp.roll(field, -2, axis)) / 12.0

def second_diff(field, axis):
    return (-jnp.roll(field, 2, axis) + 16.0 * jnp.roll(field, 1, axis) - 30.0 * field + 16.0 * jnp.roll(field, -1, axis) - jnp.roll(field, -2, axis)) / 12.0

def surface(grad_a, grad_b, curve_aa, curve_bb, curve_ab):
    tan_a = (1.0 + grad_a[0], grad_a[1], grad_a[2])
    tan_b = (grad_b[0], 1.0 + grad_b[1], grad_b[2])
    normal = (tan_a[1] * tan_b[2] - tan_a[2] * tan_b[1], tan_a[2] * tan_b[0] - tan_a[0] * tan_b[2], tan_a[0] * tan_b[1] - tan_a[1] * tan_b[0])
    area_stretch_factor = jnp.sqrt(normal[0] * normal[0] + normal[1] * normal[1] + normal[2] * normal[2])
    unit = (normal[0] / area_stretch_factor, normal[1] / area_stretch_factor, normal[2] / area_stretch_factor)
    first_edge_term = tan_a[0] * tan_a[0] + tan_a[1] * tan_a[1] + tan_a[2] * tan_a[2]
    first_f = tan_a[0] * tan_b[0] + tan_a[1] * tan_b[1] + tan_a[2] * tan_b[2]
    first_g = tan_b[0] * tan_b[0] + tan_b[1] * tan_b[1] + tan_b[2] * tan_b[2]
    second_l = curve_aa[0] * unit[0] + curve_aa[1] * unit[1] + curve_aa[2] * unit[2]
    second_m = curve_ab[0] * unit[0] + curve_ab[1] * unit[1] + curve_ab[2] * unit[2]
    second_n = curve_bb[0] * unit[0] + curve_bb[1] * unit[1] + curve_bb[2] * unit[2]
    curvature = (first_edge_term * second_n - 2.0 * first_f * second_m + first_g * second_l) / (2.0 * area_stretch_factor * area_stretch_factor)
    omega = (grad_a[3] / area_stretch_factor, grad_b[3] / area_stretch_factor)
    return (unit, curvature, omega)

def reference(shift_plane, height, dipole):
    fields = jnp.concatenate([shift_plane, height[None], dipole[None]], 0)
    grad_a = first_diff(fields, 1)
    grad_b = first_diff(fields, 2)
    curve_aa = second_diff(fields[:3], 1)
    curve_bb = second_diff(fields[:3], 2)
    curve_ab = first_diff(first_diff(fields[:3], 2), 1)
    unit, curvature, omega = surface(grad_a, grad_b, curve_aa, curve_bb, curve_ab)
    spec_one = jnp.fft.fft2(omega[0])
    spec_two = jnp.fft.fft2(omega[1])
    freq_one = jnp.fft.fftfreq(NA).astype(omega[0].dtype)[:, None]
    freq_two = jnp.fft.fftfreq(NB).astype(omega[0].dtype)[None, :]
    radius = jnp.sqrt(freq_one * freq_one + freq_two * freq_two)
    live = (jnp.abs(freq_one) < 0.5) & (jnp.abs(freq_two) < 0.5) & (radius > 0.0)
    factor = jnp.where(live, 0.5 / jnp.where(live, radius, 1.0), 0.0)
    summed = factor * (freq_one * spec_one + freq_two * spec_two)
    speed_hat = summed * -1j
    speed = jnp.real(jnp.fft.ifft2(speed_hat)).astype(height.dtype)
    velocity_update = jnp.stack([speed * unit[0], speed * unit[1], speed * unit[2]])
    dipole_update = -2.0 * 0.5 * 0.5 * height + 0.3 * curvature + 0.5 * speed * speed
    return (velocity_update.astype(jnp.float32), dipole_update.astype(jnp.float32))
```

```python
import functools

import jax
import jax.numpy as jnp
import numpy as np
from jax import lax
from jax.experimental import pallas as pl
from jax.experimental.pallas import tpu as pltpu
from jax.sharding import PartitionSpec as P

LANE = 128
SUB = 8
F32 = jnp.float32
BF16 = jnp.bfloat16
VMEM_LIMIT = 60 * 1024 * 1024


def times_unit(value, turn, count):
    re, im = value
    turn %= count
    if turn == 0:
        return value
    if 4 * turn == count:
        return (-im, re)
    if 2 * turn == count:
        return (-re, -im)
    if 4 * turn == 3 * count:
        return (im, -re)
    c = float(np.cos(2 * np.pi * turn / count))
    s = float(np.sin(2 * np.pi * turn / count))
    if 8 * turn % count == 0:
        h = abs(c)
        if c * s > 0:
            out = (h * (re - im), h * (re + im))
        else:
            out = (h * (re + im), h * (im - re))
        if c < 0:
            out = (-out[0], -out[1])
        return out
    return (c * re - s * im, c * im + s * re)


def add(p, q):
    return (p[0] + q[0], p[1] + q[1])


def sub(p, q):
    return (p[0] - q[0], p[1] - q[1])


def fft_list(vals, sign):
    n = len(vals)
    if n == 1:
        return vals
    if n == 2:
        return [add(vals[0], vals[1]), sub(vals[0], vals[1])]
    quarter = n // 4
    parts = [fft_list(vals[j::4], sign) for j in range(4)]
    out = [None] * n
    for k in range(quarter):
        t = [times_unit(parts[j][k], sign * j * k, n) for j in range(4)]
        a, b = add(t[0], t[2]), sub(t[0], t[2])
        c, d = add(t[1], t[3]), sub(t[1], t[3])
        d = (-d[1], d[0]) if sign > 0 else (d[1], -d[0])
        out[k] = add(a, c)
        out[k + quarter] = add(b, d)
        out[k + 2 * quarter] = sub(a, c)
        out[k + 3 * quarter] = sub(b, d)
    return out


def rfft_list(vals):
    n = len(vals)
    if n == 2:
        return [(vals[0] + vals[1], None), (vals[0] - vals[1], None)]
    even, odd = rfft_list(vals[0::2]), rfft_list(vals[1::2])
    out = [None] * (n // 2 + 1)
    out[0] = (even[0][0] + odd[0][0], None)
    out[n // 2] = (even[0][0] - odd[0][0], None)
    for k in range(1, n // 4):
        t = times_unit(odd[k], -k, n)
        out[k] = add(even[k], t)
        low = sub(even[k], t)
        out[n // 2 - k] = (low[0], -low[1])
    out[n // 4] = (even[n // 4][0], -odd[n // 4][0])
    return out


def irfft_list(spec):
    n = 2 * (len(spec) - 1)
    if n == 2:
        return [spec[0][0] + spec[1][0], spec[0][0] - spec[1][0]]
    q = n // 4
    even, odd = [None] * (q + 1), [None] * (q + 1)
    even[0] = (spec[0][0] + spec[n // 2][0], None)
    odd[0] = (spec[0][0] - spec[n // 2][0], None)
    for k in range(1, q):
        other = (spec[n // 2 - k][0], -spec[n // 2 - k][1])
        even[k] = add(spec[k], other)
        odd[k] = times_unit(sub(spec[k], other), k, n)
    even[q] = (2.0 * spec[q][0], None)
    odd[q] = (-2.0 * spec[q][1], None)
    out = [None] * n
    out[0::2] = irfft_list(even)
    out[1::2] = irfft_list(odd)
    return out


def hi_lo(table):
    hi = table.astype(np.float32).astype(jnp.bfloat16)
    lo = (table - hi.astype(np.float64)).astype(np.float32).astype(jnp.bfloat16)
    return hi, lo


def row_numbers(length):
    outer = length // LANE
    blocks, half = outer // 2, LANE // 2
    number = np.arange(blocks)[:, None] + outer * np.arange(LANE)[None, :]
    number[0, :half] = outer * np.arange(half)
    number[0, half:] = blocks + outer * np.arange(half)
    return number


def row_tables(length):
    outer = length // LANE
    blocks, half = outer // 2, LANE // 2
    number = row_numbers(length)
    place = np.arange(LANE)
    ahead = np.zeros((blocks, 2 * LANE, 2 * LANE))
    back = np.zeros((blocks, 2 * LANE, 2 * LANE))
    for k in range(blocks):
        theta = 2 * np.pi * ((number[k][:, None] * place[None, :]) % length) / length
        c, s = np.cos(theta), np.sin(theta)
        if k:
            ahead[k] = np.block([[c, s], [-s, c]])
            back[k] = np.block([[c.T, -s.T], [s.T, c.T]])
        else:
            zero = np.zeros((half, LANE))
            ahead[0] = np.block(
                [[c[:half], zero], [zero, c[half:]], [-s[:half], zero], [zero, -s[half:]]]
            )
            weight = np.full((half, 1), 2.0)
            weight[0] = 1.0
            back[0] = np.block(
                [
                    [(weight * c[:half]).T, zero.T, -(weight * s[:half]).T, zero.T],
                    [zero.T, 2 * c[half:].T, zero.T, -2 * s[half:].T],
                ]
            )
    def packed(t):
        hi, lo = hi_lo(t)
        return np.concatenate([hi, lo, hi], axis=-1)

    return packed(ahead), packed(back)


def col_tables(length, scale):
    outer = length // LANE
    place = np.arange(LANE)
    theta = 2 * np.pi * ((place[:, None] * place[None, :]) % LANE) / LANE
    c, s = np.cos(theta), np.sin(theta)
    ahead = np.block([[c, -s], [s, c]])
    turned = np.block([[s, -c], [c, s]])
    back = turned * scale
    def packed(t):
        hi, lo = hi_lo(t)
        return np.concatenate([hi, lo, hi], axis=0)

    first = np.arange(outer)[:, None]
    angle = 2 * np.pi * ((first * place[None, :]) % length) / length
    twist = np.stack([np.cos(angle), np.sin(angle)]).astype(np.float32)
    twist = np.ascontiguousarray(np.broadcast_to(twist[:, :, None, :], (2, outer, SUB, LANE)))
    number = first + outer * place[None, :]
    signed = np.where(number >= length // 2, number - length, number)
    freq = (signed / length).astype(np.float32)
    live = np.where(number == length // 2, 0.0, 0.5).astype(np.float32)
    freq = np.stack([freq, live])[:, :, None, :]
    freq = np.ascontiguousarray(np.broadcast_to(freq, (2, outer, SUB, LANE)))
    return packed(ahead), packed(back), twist, freq


def split(x):
    hi = x.astype(BF16)
    return hi, (x - hi.astype(F32)).astype(BF16)


def params(**more):
    return pltpu.CompilerParams(vmem_limit_bytes=VMEM_LIMIT, **more)


def whole(array):
    zeros = (0,) * array.ndim
    return pl.BlockSpec(array.shape, lambda *_: zeros, pipeline_mode=pl.Buffered(1))


def row_kernel(x_ref, w_ref, o_ref, s_ref):
    sides, _, rows, width = x_ref.shape
    per = width // LANE
    outer = sides * per
    blocks = outer // 2

    for field in range(2):

        def short(g, _, field=field):
            at = pl.ds(pl.multiple_of(g * SUB, SUB), SUB)
            vals = [
                x_ref[a // per, field, at, (a % per) * LANE : (a % per + 1) * LANE]
                for a in range(outer)
            ]
            spec = rfft_list(vals)
            to = pl.ds(pl.multiple_of(field * rows + g * SUB, SUB), SUB)
            s_ref[0, to, :LANE] = spec[0][0]
            s_ref[0, to, LANE:] = spec[blocks][0]
            for k in range(1, blocks):
                s_ref[k, to, :LANE] = spec[k][0]
                s_ref[k, to, LANE:] = spec[k][1]
            return 0

        lax.fori_loop(0, rows // SUB, short, 0)

    def long(k, _):
        hi, lo = split(s_ref[k])
        y = lax.dot_general(
            w_ref[k],
            jnp.concatenate([hi, hi, lo], axis=1),
            (((1,), (1,)), ((), ())),
            preferred_element_type=F32,
        )
        for field in range(2):
            for part in range(2):
                o_ref[k, 2 * field + part] = y[
                    part * LANE : (part + 1) * LANE, field * rows : (field + 1) * rows
                ]
        return 0

    lax.fori_loop(0, blocks, long, 0, unroll=2)


def row_forward(x, table):
    sides, _, rows, width = x.shape
    blocks = sides * width // LANE // 2
    step = LANE if rows % LANE == 0 else rows
    return pl.pallas_call(
        row_kernel,
        grid=(rows // step,),
        in_specs=[
            pl.BlockSpec((sides, 2, step, width), lambda i: (0, 0, i, 0)),
            whole(table),
        ],
        out_specs=pl.BlockSpec((blocks, 4, LANE, step), lambda i: (0, 0, 0, i)),
        out_shape=jax.ShapeDtypeStruct((blocks, 4, LANE, rows), F32),
        scratch_shapes=[pltpu.VMEM((blocks, 2 * step, 2 * LANE), F32)],
        compiler_params=params(),
        name="row_forward",
    )(x, table)


def col_kernel(x_ref, f2_ref, wf_ref, wb_ref, tw_ref, f1_ref, o_ref, a_ref, z_ref, *, chunk):
    sources, _, _, count, length = x_ref.shape
    per = length // LANE
    outer = tw_ref.shape[1]

    for field in range(2):

        def short(g, _, field=field):
            at = pl.ds(pl.multiple_of(g * SUB, SUB), SUB)

            def part(a, which):
                lanes = slice((a % per) * LANE, (a % per + 1) * LANE)
                return x_ref[a // per, 0, 2 * field + which, at, lanes]

            spec = fft_list([(part(a, 0), part(a, 1)) for a in range(outer)], -1)
            for k in range(outer):
                re, im = spec[k]
                if k:
                    c, s = tw_ref[0, k], tw_ref[1, k]
                    re, im = (re * c + im * s, im * c - re * s)
                a_ref[field, k, at, :LANE] = re
                a_ref[field, k, at, LANE:] = im
            return 0

        lax.fori_loop(0, count // SUB, short, 0)

    f2 = f2_ref[0]
    f2_square = jnp.maximum(f2 * f2, 1e-30)

    def long(j, _):
        at = pl.ds(j * chunk, chunk)

        def product(x, w_ref):
            hi, lo = split(x.reshape(chunk * count, 2 * LANE))
            return jnp.dot(
                jnp.concatenate([hi, hi, lo], axis=1), w_ref[...], preferred_element_type=F32
            ).reshape(chunk, count, 2 * LANE)

        y0 = product(a_ref[0, at], wf_ref)
        y1 = product(a_ref[1, at], wf_ref)
        f1 = f1_ref[0, at][:, :1]
        factor = f1_ref[1, at][:, :1] * lax.rsqrt(f1 * f1 + f2_square[None])
        m0, m1 = factor * f1, factor * f2[None]
        m0 = jnp.concatenate([m0, m0], axis=-1)
        m1 = jnp.concatenate([m1, m1], axis=-1)
        z_ref[at] = product(m0 * y0 + m1 * y1, wb_ref)
        return 0

    lax.fori_loop(0, outer // chunk, long, 0)

    def last(g, _):
        at = pl.ds(pl.multiple_of(g * SUB, SUB), SUB)
        vals = []
        for k in range(outer):
            re, im = z_ref[k, at, :LANE], z_ref[k, at, LANE:]
            if k:
                c, s = tw_ref[0, k], tw_ref[1, k]
                re, im = (re * c - im * s, im * c + re * s)
            vals.append((re, im))
        res = fft_list(vals, 1)
        for a in range(outer):
            lanes = slice((a % per) * LANE, (a % per + 1) * LANE)
            o_ref[a // per, 0, 0, at, lanes] = res[a][0]
            o_ref[a // per, 0, 1, at, lanes] = res[a][1]
        return 0

    lax.fori_loop(0, count // SUB, last, 0)


def col_stage(x, f2, tables):
    sources, u, _, n, rows = x.shape
    outer = sources * rows // LANE
    step = n
    while step > 32 and step % 2 == 0:
        step //= 2
    chunk = max(1, min(outer, 256 // step))
    return pl.pallas_call(
        functools.partial(col_kernel, chunk=chunk),
        grid=(u, n // step),
        in_specs=[
            pl.BlockSpec((sources, 1, 4, step, rows), lambda i, j: (0, i, 0, j, 0)),
            pl.BlockSpec((1, step, LANE), lambda i, j: (i, j, 0)),
        ]
        + [whole(t) for t in tables],
        out_specs=pl.BlockSpec((sources, 1, 2, step, rows), lambda i, j: (0, i, 0, j, 0)),
        out_shape=jax.ShapeDtypeStruct((sources, u, 2, n, rows), F32),
        scratch_shapes=[
            pltpu.VMEM((2, outer, step, 2 * LANE), F32),
            pltpu.VMEM((outer, step, 2 * LANE), F32),
        ],
        compiler_params=params(),
        name="col_stage",
    )(x, f2, *tables)


def back_kernel(x_ref, w_ref, o_ref, z_ref, t_ref):
    blocks, _, _, rows = x_ref.shape
    sides, _, width = o_ref.shape
    outer = 2 * blocks
    per = width // LANE

    def long(k, _):
        hi, lo = split(x_ref[k].reshape(2 * LANE, rows))
        z_ref[k] = jnp.dot(
            w_ref[k], jnp.concatenate([hi, hi, lo], axis=0), preferred_element_type=F32
        )
        return 0

    lax.fori_loop(0, blocks, long, 0, unroll=2)

    def short(g, _):
        at = pl.ds(pl.multiple_of(g * SUB, SUB), SUB)
        low = pl.ds(pl.multiple_of(LANE + g * SUB, SUB), SUB)
        spec = [(z_ref[0, at], None)]
        spec += [(z_ref[k, at], z_ref[k, low]) for k in range(1, blocks)]
        spec += [(z_ref[0, low], None)]
        res = irfft_list(spec)
        for a in range(outer):
            t_ref[a, at] = res[a]
        return 0

    lax.fori_loop(0, LANE // SUB, short, 0)

    for a in range(outer):
        lanes = slice((a % per) * LANE, (a % per + 1) * LANE)
        o_ref[a // per, :, lanes] = t_ref[a].T


def row_back(x, table, sides):
    blocks, _, _, rows = x.shape
    width = 2 * blocks * LANE // sides
    step = LANE if rows % LANE == 0 else rows
    return pl.pallas_call(
        back_kernel,
        grid=(rows // step,),
        in_specs=[
            pl.BlockSpec((blocks, 2, LANE, step), lambda i: (0, 0, 0, i)),
            whole(table),
        ],
        out_specs=pl.BlockSpec((sides, step, width), lambda i: (0, i, 0)),
        out_shape=jax.ShapeDtypeStruct((sides, rows, width), F32),
        scratch_shapes=[
            pltpu.VMEM((blocks, 2 * LANE, step), F32),
            pltpu.VMEM((2 * blocks, LANE, step), F32),
        ],
        compiler_params=params(),
        name="row_back",
    )(x, table)


def diff_one(m2, m1, p1, p2):
    return (p1 - m1) * (2.0 / 3.0) - (p2 - m2) * (1.0 / 12.0)


def diff_two(m2, m1, zero, p1, p2):
    return (p1 + m1) * (4.0 / 3.0) - (p2 + m2) * (1.0 / 12.0) - 2.5 * zero


def normal_of(ga, gb):
    a = (1.0 + ga[0], ga[1], ga[2])
    b = (gb[0], 1.0 + gb[1], gb[2])
    normal = (
        a[1] * b[2] - a[2] * b[1],
        a[2] * b[0] - a[0] * b[2],
        a[0] * b[1] - a[1] * b[0],
    )
    return a, b, normal


def dot3(p, q):
    return p[0] * q[0] + p[1] * q[1] + p[2] * q[2]


def fill(ext_ref, index, refs, field, edge):
    block, prev, after = refs
    rows, width = block.shape[-2:]
    top_ref, low_ref, left_ref, right_ref = edge
    i, n = pl.program_id(0), pl.num_programs(0)
    mid = slice(LANE, LANE + width)
    ext_ref[index, SUB : SUB + rows, mid] = block[field]
    ext_ref[index, :SUB, mid] = jnp.where(i == 0, top_ref[index], prev[field])
    ext_ref[index, SUB + rows :, mid] = jnp.where(i == n - 1, low_ref[index], after[field])
    lines = left_ref.shape[1]
    if lines == rows:
        ext_ref[index, SUB : SUB + rows, :LANE] = left_ref[index]
        ext_ref[index, SUB : SUB + rows, LANE + width :] = right_ref[index]
    else:
        at = pl.ds(pl.multiple_of(i * rows, SUB), rows + 2 * SUB)
        ext_ref[index, :, :LANE] = left_ref[index, at]
        ext_ref[index, :, LANE + width :] = right_ref[index, at]


def shifted(x, by, width):
    total = x.shape[-1]
    return pltpu.roll(x, (-by) % total, x.ndim - 1)[..., LANE : LANE + width]


def tiles(rows, width, body):
    wide = 2 * LANE if width % (2 * LANE) == 0 else LANE
    across = width // wide

    def step(t, _):
        r = pl.multiple_of((t // across) * SUB, SUB)
        c = pl.multiple_of((t % across) * wide, LANE)
        body(r, c, wide)
        return 0

    lax.fori_loop(0, rows // SUB * across, step, 0)


def around(ext_ref, index, r, c, wide):
    return ext_ref[index, pl.ds(r, 3 * SUB), pl.ds(c, wide + 2 * LANE)]


def vorticity_kernel(*refs):
    planes, heights, dipoles, edge = refs[0:3], refs[3:6], refs[6:9], refs[9:13]
    o_ref, ext_ref = refs[13], refs[14]
    rows, width = o_ref.shape[-2:]
    for index, (source, field) in enumerate(
        [(planes, 0), (planes, 1), (heights, 0), (dipoles, 0)]
    ):
        fill(ext_ref, index, source, field, edge)

    def body(r, c, wide):
        ga, gb = [], []
        for index in range(4):
            x = around(ext_ref, index, r, c, wide)
            tall = x[:, LANE : LANE + wide]
            ga.append(diff_one(*[tall[SUB + s : 2 * SUB + s] for s in (-2, -1, 1, 2)]))
            flat = x[SUB : 2 * SUB]
            gb.append(diff_one(*[shifted(flat, s, wide) for s in (-2, -1, 1, 2)]))
        _, _, normal = normal_of(ga, gb)
        inverse = lax.rsqrt(dot3(normal, normal))
        o_ref[0, 0, pl.ds(r, SUB), pl.ds(c, wide)] = ga[3] * inverse
        o_ref[0, 1, pl.ds(r, SUB), pl.ds(c, wide)] = gb[3] * inverse

    tiles(rows, width, body)


def geometry_kernel(*refs):
    planes, heights, edge = refs[0:3], refs[3:6], refs[6:10]
    unit_ref, base_ref, ext_ref = refs[10:13]
    rows, width = base_ref.shape[-2:]
    for index, (source, field) in enumerate([(planes, 0), (planes, 1), (heights, 0)]):
        fill(ext_ref, index, source, field, edge)

    def body(r, c, wide):
        ga, gb, caa, cbb, cab = [], [], [], [], []
        for index in range(3):
            x = around(ext_ref, index, r, c, wide)
            moved = [shifted(x, s, wide) for s in (-2, -1, 1, 2)]
            across = diff_one(*moved)
            tall = x[:, LANE : LANE + wide]
            rowed = [tall[SUB + s : 2 * SUB + s] for s in (-2, -1, 0, 1, 2)]
            ga.append(diff_one(rowed[0], rowed[1], rowed[3], rowed[4]))
            caa.append(diff_two(*rowed))
            gb.append(across[SUB : 2 * SUB])
            m = [v[SUB : 2 * SUB] for v in moved]
            cbb.append(diff_two(m[0], m[1], rowed[2], m[2], m[3]))
            cab.append(diff_one(*[across[SUB + s : 2 * SUB + s] for s in (-2, -1, 1, 2)]))
            if index == 2:
                height = rowed[2]
        a, b, normal = normal_of(ga, gb)
        inverse = lax.rsqrt(dot3(normal, normal))
        top = (
            dot3(a, a) * dot3(cbb, normal)
            - 2.0 * dot3(a, b) * dot3(cab, normal)
            + dot3(b, b) * dot3(caa, normal)
        )
        curvature = 0.5 * top * (inverse * inverse * inverse)
        at = (pl.ds(r, SUB), pl.ds(c, wide))
        for axis in range(3):
            unit_ref[(axis,) + at] = normal[axis] * inverse
        base_ref[at] = 0.3 * curvature - 0.5 * height

    tiles(rows, width, body)


def row_step(rows):
    step = 64
    while rows % step:
        step //= 2
    return step


def block_specs(count, step, rows, width):
    per, total = step // SUB, rows // SUB
    return [
        pl.BlockSpec((count, step, width), lambda i: (0, i, 0)),
        pl.BlockSpec((count, SUB, width), lambda i: (0, jnp.maximum(i * per - 1, 0), 0)),
        pl.BlockSpec((count, SUB, width), lambda i: (0, jnp.minimum((i + 1) * per, total - 1), 0)),
    ]


def vorticity_stage(planes, height, dipole, edge, sides):
    _, rows, width = planes.shape
    part = rows // sides
    step = row_step(part)
    rim = lambda: pl.BlockSpec((4, step, LANE), lambda i: (0, i, 0))
    return pl.pallas_call(
        vorticity_kernel,
        grid=(rows // step,),
        in_specs=block_specs(2, step, rows, width)
        + block_specs(1, step, rows, width) * 2
        + [whole(edge[0]), whole(edge[1]), rim(), rim()],
        out_specs=pl.BlockSpec(
            (1, 2, step, width), lambda i: (i // (part // step), 0, i % (part // step), 0)
        ),
        out_shape=jax.ShapeDtypeStruct((sides, 2, part, width), F32),
        scratch_shapes=[pltpu.VMEM((4, step + 2 * SUB, width + 2 * LANE), F32)],
        compiler_params=params(),
        name="vorticity_stage",
    )(*[planes] * 3, *[height[None]] * 3, *[dipole[None]] * 3, *edge)


def geometry_stage(planes, height, edge):
    _, rows, width = planes.shape
    step = row_step(rows)
    return pl.pallas_call(
        geometry_kernel,
        grid=(rows // step,),
        in_specs=block_specs(2, step, rows, width)
        + block_specs(1, step, rows, width)
        + [whole(e) for e in edge],
        out_specs=[
            pl.BlockSpec((3, step, width), lambda i: (0, i, 0)),
            pl.BlockSpec((step, width), lambda i: (i, 0)),
        ],
        out_shape=[
            jax.ShapeDtypeStruct((3, rows, width), F32),
            jax.ShapeDtypeStruct((rows, width), F32),
        ],
        scratch_shapes=[pltpu.VMEM((3, step + 2 * SUB, width + 2 * LANE), F32)],
        compiler_params=params(),
        cost_estimate=pl.CostEstimate(
            flops=200 * rows * width, bytes_accessed=7 * 4 * rows * width, transcendentals=rows * width
        ),
        name="geometry_stage",
    )(*[planes] * 3, *[height[None]] * 3, *edge)


def final_kernel(speed_ref, unit_ref, base_ref, velocity_ref, update_ref):
    speed = speed_ref[...]
    for axis in range(3):
        velocity_ref[axis] = speed * unit_ref[axis]
    update_ref[...] = base_ref[...] + 0.5 * speed * speed


def final_stage(speed, unit, base):
    rows, width = base.shape
    step = row_step(rows)
    three = lambda: pl.BlockSpec((3, step, width), lambda i: (0, i, 0))
    one = lambda: pl.BlockSpec((step, width), lambda i: (i, 0))
    return pl.pallas_call(
        final_kernel,
        grid=(rows // step,),
        in_specs=[one(), three(), one()],
        out_specs=[three(), one()],
        out_shape=[
            jax.ShapeDtypeStruct((3, rows, width), F32),
            jax.ShapeDtypeStruct((rows, width), F32),
        ],
        compiler_params=params(),
        name="final_stage",
    )(speed, unit, base)


def both_ways(last, initial, axis):
    devices = lax.axis_size(axis)
    up = [(i, (i + 1) % devices) for i in range(devices)]
    down = [(j, i) for i, j in up]
    return lax.ppermute(last, axis, up), lax.ppermute(initial, axis, down)


def local(shift_plane, height, dipole):
    _, rows, width = shift_plane.shape
    tr, tc = lax.axis_size("tr"), lax.axis_size("tc")
    devices = tr * tc
    row_count, col_count = rows * tr, width * tc
    part = rows // tc

    def cut(a, b, dim):
        pieces = [shift_plane, height[None], dipole[None]]
        return jnp.concatenate([lax.slice_in_dim(p, a, b, axis=dim) for p in pieces], 0)

    left, right = both_ways(cut(width - LANE, width, 2), cut(0, LANE, 2), "tc")
    top, low = both_ways(cut(rows - SUB, rows, 1), cut(0, SUB, 1), "tr")
    vorticity = vorticity_stage(
        shift_plane, height, dipole, (top, low, left, right), tc
    )
    sheet = lax.all_to_all(vorticity, "tc", split_axis=0, concat_axis=0, tiled=True)
    row_table, back_table = row_tables(col_count)
    spec = row_forward(sheet, row_table)
    blocks = spec.shape[0]
    n = blocks * LANE // devices
    u = max(1, n // LANE)
    n = n // u
    pieces = LANE // n
    spec = spec.reshape(blocks, 4, pieces, n, part)
    spec = jnp.swapaxes(spec, 1, 2).reshape(devices, u, 4, n, part)
    columns = lax.all_to_all(spec, ("tr", "tc"), split_axis=0, concat_axis=0, tiled=True)

    ends = jnp.stack([top[:3], low[:3]])
    left_ends, right_ends = both_ways(ends[..., width - LANE :], ends[..., :LANE], "tc")
    edge = (
        top[:3],
        low[:3],
        jnp.concatenate([left_ends[0], left[:3], left_ends[1]], 1),
        jnp.concatenate([right_ends[0], right[:3], right_ends[1]], 1),
    )
    unit, base = geometry_stage(shift_plane, height, edge)

    direct = part % LANE == 0
    if not direct:
        columns = columns.transpose(1, 2, 3, 0, 4).reshape(1, u, 4, n, row_count)
    number = row_numbers(col_count).reshape(-1)
    signed = np.where(number >= col_count // 2, number - col_count, number)
    freq = (signed / col_count).astype(np.float32)
    freq = np.ascontiguousarray(np.broadcast_to(freq[:, None], (freq.size, LANE)))
    place = lax.axis_index(("tr", "tc")) * (u * n)
    mine = lax.dynamic_slice_in_dim(jnp.asarray(freq), place, u * n, 0).reshape(u, n, LANE)
    tables = col_tables(row_count, 1.0 / (row_count * col_count))
    partial = col_stage(columns, mine, tables)
    if not direct:
        partial = partial.reshape(u, 2, n, devices, part).transpose(3, 0, 1, 2, 4)
    back = lax.all_to_all(partial, ("tr", "tc"), split_axis=0, concat_axis=0, tiled=True)
    back = back.reshape(blocks, pieces, 2, n, part)
    back = jnp.swapaxes(back, 1, 2).reshape(blocks, 2, LANE, part)
    speed_rows = row_back(back, back_table, tc)
    speed = lax.all_to_all(speed_rows, "tc", split_axis=0, concat_axis=0, tiled=True)
    velocity_update, dipole_update = final_stage(speed.reshape(rows, width), unit, base)
    return (velocity_update, dipole_update)


def solution(mesh):
    in_specs = (
        P(None, ("groups", "tr"), "tc"),
        P(("groups", "tr"), "tc"),
        P(("groups", "tr"), "tc"),
    )
    out_specs = (P(None, ("groups", "tr"), "tc"), P(("groups", "tr"), "tc"))
    return jax.shard_map(local, mesh=mesh, in_specs=in_specs, out_specs=out_specs, check_vma=False)
```

```python
import functools

import jax
import jax.numpy as jnp
import numpy as np
from jax import lax
from jax.experimental import pallas as pl
from jax.experimental.pallas import tpu as pltpu
from jax.sharding import PartitionSpec as P

LANE = 128
SUB = 8
MANY = 4
RIM = 2
F32 = jnp.float32
BF16 = jnp.bfloat16
VMEM_LIMIT = 60 * 1024 * 1024


def times_unit(value, turn, count):
    re, im = value
    turn %= count
    if turn == 0:
        return value
    if 4 * turn == count:
        return (-im, re)
    if 2 * turn == count:
        return (-re, -im)
    if 4 * turn == 3 * count:
        return (im, -re)
    c = float(np.cos(2 * np.pi * turn / count))
    s = float(np.sin(2 * np.pi * turn / count))
    if 8 * turn % count == 0:
        h = abs(c)
        if c * s > 0:
            out = (h * (re - im), h * (re + im))
        else:
            out = (h * (re + im), h * (im - re))
        if c < 0:
            out = (-out[0], -out[1])
        return out
    return (c * re - s * im, c * im + s * re)


def add(p, q):
    return (p[0] + q[0], p[1] + q[1])


def sub(p, q):
    return (p[0] - q[0], p[1] - q[1])


def fft_list(vals, sign):
    n = len(vals)
    if n == 1:
        return vals
    if n == 2:
        return [add(vals[0], vals[1]), sub(vals[0], vals[1])]
    quarter = n // 4
    parts = [fft_list(vals[j::4], sign) for j in range(4)]
    out = [None] * n
    for k in range(quarter):
        t = [times_unit(parts[j][k], sign * j * k, n) for j in range(4)]
        a, b = add(t[0], t[2]), sub(t[0], t[2])
        c, d = add(t[1], t[3]), sub(t[1], t[3])
        d = (-d[1], d[0]) if sign > 0 else (d[1], -d[0])
        out[k] = add(a, c)
        out[k + quarter] = add(b, d)
        out[k + 2 * quarter] = sub(a, c)
        out[k + 3 * quarter] = sub(b, d)
    return out


def rfft_list(vals):
    n = len(vals)
    if n == 2:
        return [(vals[0] + vals[1], None), (vals[0] - vals[1], None)]
    even, odd = rfft_list(vals[0::2]), rfft_list(vals[1::2])
    out = [None] * (n // 2 + 1)
    out[0] = (even[0][0] + odd[0][0], None)
    out[n // 2] = (even[0][0] - odd[0][0], None)
    for k in range(1, n // 4):
        t = times_unit(odd[k], -k, n)
        out[k] = add(even[k], t)
        low = sub(even[k], t)
        out[n // 2 - k] = (low[0], -low[1])
    out[n // 4] = (even[n // 4][0], -odd[n // 4][0])
    return out


def irfft_list(spec):
    n = 2 * (len(spec) - 1)
    if n == 2:
        return [spec[0][0] + spec[1][0], spec[0][0] - spec[1][0]]
    q = n // 4
    even, odd = [None] * (q + 1), [None] * (q + 1)
    even[0] = (spec[0][0] + spec[n // 2][0], None)
    odd[0] = (spec[0][0] - spec[n // 2][0], None)
    for k in range(1, q):
        other = (spec[n // 2 - k][0], -spec[n // 2 - k][1])
        even[k] = add(spec[k], other)
        odd[k] = times_unit(sub(spec[k], other), k, n)
    even[q] = (2.0 * spec[q][0], None)
    odd[q] = (-2.0 * spec[q][1], None)
    out = [None] * n
    out[0::2] = irfft_list(even)
    out[1::2] = irfft_list(odd)
    return out


def hi_lo(table):
    hi = table.astype(np.float32).astype(jnp.bfloat16)
    lo = (table - hi.astype(np.float64)).astype(np.float32).astype(jnp.bfloat16)
    return hi, lo


def row_numbers(length):
    outer = length // LANE
    blocks, half = outer // 2, LANE // 2
    number = np.arange(blocks)[:, None] + outer * np.arange(LANE)[None, :]
    number[0, :half] = outer * np.arange(half)
    number[0, half:] = blocks + outer * np.arange(half)
    return number


def row_tables(length):
    outer = length // LANE
    blocks, half = outer // 2, LANE // 2
    number = row_numbers(length)
    place = np.arange(LANE)
    ahead = np.zeros((blocks, 2 * LANE, 2 * LANE))
    back = np.zeros((blocks, 2 * LANE, 2 * LANE))
    for k in range(blocks):
        theta = 2 * np.pi * ((number[k][:, None] * place[None, :]) % length) / length
        c, s = np.cos(theta), np.sin(theta)
        if k:
            ahead[k] = np.block([[c, s], [-s, c]])
            back[k] = np.block([[c.T, -s.T], [s.T, c.T]])
        else:
            zero = np.zeros((half, LANE))
            ahead[0] = np.block(
                [[c[:half], zero], [zero, c[half:]], [-s[:half], zero], [zero, -s[half:]]]
            )
            weight = np.full((half, 1), 2.0)
            weight[0] = 1.0
            back[0] = np.block(
                [
                    [(weight * c[:half]).T, zero.T, -(weight * s[:half]).T, zero.T],
                    [zero.T, 2 * c[half:].T, zero.T, -2 * s[half:].T],
                ]
            )
    def packed(t):
        return np.concatenate(hi_lo(t), axis=1)

    return packed(ahead), packed(back)


def col_tables(length, scale):
    outer = length // LANE
    place = np.arange(LANE)
    theta = 2 * np.pi * ((place[:, None] * place[None, :]) % LANE) / LANE
    c, s = np.cos(theta), np.sin(theta)
    ahead = np.block([[c, -s], [s, c]])
    turned = np.block([[s, -c], [c, s]])
    back = turned * scale
    def packed(t):
        hi, lo = hi_lo(t)
        return np.concatenate([hi, lo, hi], axis=0)

    first = np.arange(outer)[:, None]
    angle = 2 * np.pi * ((first * place[None, :]) % length) / length
    twist = np.stack([np.cos(angle), np.sin(angle)]).astype(np.float32)
    twist = np.ascontiguousarray(np.broadcast_to(twist[:, :, None, :], (2, outer, SUB, LANE)))
    number = first + outer * place[None, :]
    signed = np.where(number >= length // 2, number - length, number)
    freq = (signed / length).astype(np.float32)
    live = np.where(number == length // 2, 0.0, 0.5).astype(np.float32)
    freq = np.stack([freq, live])[:, :, None, :]
    freq = np.ascontiguousarray(np.broadcast_to(freq, (2, outer, SUB, LANE)))
    return packed(ahead), packed(back), twist, freq


def split(x):
    hi = x.astype(BF16)
    return hi, (x - hi.astype(F32)).astype(BF16)


def params(**more):
    return pltpu.CompilerParams(vmem_limit_bytes=VMEM_LIMIT, **more)


def whole(array):
    zeros = (0,) * array.ndim
    return pl.BlockSpec(array.shape, lambda *_: zeros, pipeline_mode=pl.Buffered(1))


def row_kernel(me_ref, *refs):
    x_refs, (w_ref, o_ref, s_ref) = refs[:-3], refs[-3:]
    sides = len(x_refs)
    for me in range(sides):

        @pl.when(me_ref[0] == me)
        def _(me=me):
            row_short([x_refs[(me - side) % sides] for side in range(sides)], s_ref)

    row_long(w_ref, o_ref, s_ref, x_refs[0].shape[2])


def row_short(x_refs, s_ref):
    _, per, rows, _ = x_refs[0].shape
    outer = len(x_refs) * per
    blocks = outer // 2

    for field in range(2):

        def short(g, _, field=field):
            at = pl.ds(pl.multiple_of(g * SUB, SUB), SUB)
            vals = [x_refs[a // per][field, a % per, at] for a in range(outer)]
            spec = rfft_list(vals)
            to = pl.ds(pl.multiple_of(field * rows + g * SUB, SUB), SUB)
            s_ref[0, to, :LANE] = spec[0][0]
            s_ref[0, to, LANE:] = spec[blocks][0]
            for k in range(1, blocks):
                s_ref[k, to, :LANE] = spec[k][0]
                s_ref[k, to, LANE:] = spec[k][1]
            return 0

        lax.fori_loop(0, rows // SUB, short, 0)


def three(w, x, dims):
    hi, lo = split(x)
    out = w.shape[0] // 2
    both = lax.dot_general(w, hi, dims, preferred_element_type=F32)
    rest = lax.dot_general(w[:out], lo, dims, preferred_element_type=F32)
    return both[:out] + (both[out:] + rest)


def row_long(w_ref, o_ref, s_ref, rows):
    def long(k, _):
        y = three(w_ref[k], s_ref[k], (((1,), (1,)), ((), ())))
        for field in range(2):
            for part in range(2):
                o_ref[k, 2 * field + part] = y[
                    part * LANE : (part + 1) * LANE, field * rows : (field + 1) * rows
                ]
        return 0

    lax.fori_loop(0, s_ref.shape[0], long, 0, unroll=4)


def row_forward(pieces, me, table):
    _, per, rows, _ = pieces[0].shape
    blocks = len(pieces) * per // 2
    step = LANE if rows % LANE == 0 else rows
    return pl.pallas_call(
        row_kernel,
        grid_spec=pltpu.PrefetchScalarGridSpec(
            num_scalar_prefetch=1,
            grid=(rows // step,),
            in_specs=[pl.BlockSpec((2, per, step, LANE), lambda i, _: (0, 0, i, 0)) for _ in pieces]
            + [whole(table)],
            out_specs=pl.BlockSpec((blocks, 4, LANE, step), lambda i, _: (0, 0, 0, i)),
            scratch_shapes=[pltpu.VMEM((blocks, 2 * step, 2 * LANE), F32)],
        ),
        out_shape=jax.ShapeDtypeStruct((blocks, 4, LANE, rows), F32),
        compiler_params=params(),
        name="row_forward",
    )(me[None], *pieces, table)


def col_kernel(x_ref, f2_ref, wf_ref, wb_ref, tw_ref, f1_ref, o_ref, a_ref, z_ref, *, chunk):
    sources, _, _, count, length = x_ref.shape
    per = length // LANE
    outer = tw_ref.shape[1]

    for field in range(2):

        def short(g, _, field=field):
            at = pl.ds(pl.multiple_of(g * SUB, SUB), SUB)

            def part(a, which):
                lanes = slice((a % per) * LANE, (a % per + 1) * LANE)
                return x_ref[a // per, 0, 2 * field + which, at, lanes]

            spec = fft_list([(part(a, 0), part(a, 1)) for a in range(outer)], -1)
            for k in range(outer):
                re, im = spec[k]
                if k:
                    c, s = tw_ref[0, k], tw_ref[1, k]
                    re, im = (re * c + im * s, im * c - re * s)
                a_ref[field, k, at, :LANE] = re
                a_ref[field, k, at, LANE:] = im
            return 0

        lax.fori_loop(0, count // SUB, short, 0)

    f2 = f2_ref[0]
    f2_square = jnp.maximum(f2 * f2, 1e-30)

    def long(j, _):
        at = pl.ds(j * chunk, chunk)

        def product(x, w_ref):
            hi, lo = split(x.reshape(chunk * count, 2 * LANE))
            return jnp.dot(
                jnp.concatenate([hi, hi, lo], axis=1), w_ref[...], preferred_element_type=F32
            ).reshape(chunk, count, 2 * LANE)

        y0 = product(a_ref[0, at], wf_ref)
        y1 = product(a_ref[1, at], wf_ref)
        f1 = f1_ref[0, at][:, :1]
        factor = f1_ref[1, at][:, :1] * lax.rsqrt(f1 * f1 + f2_square[None])
        m0, m1 = factor * f1, factor * f2[None]
        m0 = jnp.concatenate([m0, m0], axis=-1)
        m1 = jnp.concatenate([m1, m1], axis=-1)
        z_ref[at] = product(m0 * y0 + m1 * y1, wb_ref)
        return 0

    lax.fori_loop(0, outer // chunk, long, 0)

    def last(g, _):
        at = pl.ds(pl.multiple_of(g * SUB, SUB), SUB)
        vals = []
        for k in range(outer):
            re, im = z_ref[k, at, :LANE], z_ref[k, at, LANE:]
            if k:
                c, s = tw_ref[0, k], tw_ref[1, k]
                re, im = (re * c - im * s, im * c + re * s)
            vals.append((re, im))
        res = fft_list(vals, 1)
        for a in range(outer):
            lanes = slice((a % per) * LANE, (a % per + 1) * LANE)
            o_ref[a // per, 0, 0, at, lanes] = res[a][0]
            o_ref[a // per, 0, 1, at, lanes] = res[a][1]
        return 0

    lax.fori_loop(0, count // SUB, last, 0)


def col_stage(x, f2, tables):
    sources, u, _, n, rows = x.shape
    outer = sources * rows // LANE
    step = n
    while step > 32 and step % 2 == 0:
        step //= 2
    chunk = max(1, min(outer, 1024 // step))
    return pl.pallas_call(
        functools.partial(col_kernel, chunk=chunk),
        grid=(u, n // step),
        in_specs=[
            pl.BlockSpec((sources, 1, 4, step, rows), lambda i, j: (0, i, 0, j, 0)),
            pl.BlockSpec((1, step, LANE), lambda i, j: (i, j, 0)),
        ]
        + [whole(t) for t in tables],
        out_specs=pl.BlockSpec((sources, 1, 2, step, rows), lambda i, j: (0, i, 0, j, 0)),
        out_shape=jax.ShapeDtypeStruct((sources, u, 2, n, rows), F32),
        scratch_shapes=[
            pltpu.VMEM((2, outer, step, 2 * LANE), F32),
            pltpu.VMEM((outer, step, 2 * LANE), F32),
        ],
        compiler_params=params(),
        name="col_stage",
    )(x, f2, *tables)


def back_kernel(me_ref, x_ref, w_ref, *refs):
    o_refs, (z_ref, t_ref) = refs[:-2], refs[-2:]
    blocks, _, _, rows = x_ref.shape
    sides = len(o_refs)
    per = o_refs[0].shape[0]
    outer = 2 * blocks

    def long(k, _):
        z_ref[k] = three(w_ref[k], x_ref[k].reshape(2 * LANE, rows), (((1,), (0,)), ((), ())))
        return 0

    lax.fori_loop(0, blocks, long, 0, unroll=4)

    def short(g, _):
        at = pl.ds(pl.multiple_of(g * SUB, SUB), SUB)
        low = pl.ds(pl.multiple_of(LANE + g * SUB, SUB), SUB)
        spec = [(z_ref[0, at], None)]
        spec += [(z_ref[k, at], z_ref[k, low]) for k in range(1, blocks)]
        spec += [(z_ref[0, low], None)]
        res = irfft_list(spec)
        for a in range(outer):
            t_ref[a, at] = res[a]
        return 0

    lax.fori_loop(0, LANE // SUB, short, 0)

    for me in range(sides):

        @pl.when(me_ref[0] == me)
        def _(me=me):
            for a in range(outer):
                o_refs[(a // per - me) % sides][a % per] = t_ref[a].T


def row_back(x, me, table, sides):
    blocks, _, _, rows = x.shape
    per = 2 * blocks // sides
    step = LANE if rows % LANE == 0 else rows
    return pl.pallas_call(
        back_kernel,
        grid_spec=pltpu.PrefetchScalarGridSpec(
            num_scalar_prefetch=1,
            grid=(rows // step,),
            in_specs=[
                pl.BlockSpec((blocks, 2, LANE, step), lambda i, _: (0, 0, 0, i)),
                whole(table),
            ],
            out_specs=[pl.BlockSpec((per, step, LANE), lambda i, _: (0, i, 0))] * sides,
            scratch_shapes=[
                pltpu.VMEM((blocks, 2 * LANE, step), F32),
                pltpu.VMEM((2 * blocks, LANE, step), F32),
            ],
        ),
        out_shape=[jax.ShapeDtypeStruct((per, rows, LANE), F32)] * sides,
        compiler_params=params(),
        name="row_back",
    )(me[None], x, table)


def diff_one(m2, m1, p1, p2):
    return 8.0 * (p1 - m1) - (p2 - m2)


def diff_two(m2, m1, zero, p1, p2):
    return 16.0 * (p1 + m1) - (p2 + m2) - 30.0 * zero


def normal_of(ga, gb):
    a = (12.0 + ga[0], ga[1], ga[2])
    b = (gb[0], 12.0 + gb[1], gb[2])
    normal = (
        a[1] * b[2] - a[2] * b[1],
        a[2] * b[0] - a[0] * b[2],
        a[0] * b[1] - a[1] * b[0],
    )
    return a, b, normal


def dot3(p, q):
    return p[0] * q[0] + p[1] * q[1] + p[2] * q[2]


def fill(ext_ref, index, refs, field, edge, i, n):
    block, prev, after = refs
    rows, width = block.shape[-2:]
    count = width // LANE
    top_ref, low_ref, left_ref, right_ref = edge
    for j in range(count):
        at = slice(j * LANE, (j + 1) * LANE)
        ext_ref[index, 1 + j, SUB : SUB + rows] = block[field, :, at]
        ext_ref[index, 1 + j, :SUB] = prev[field, :, at]
        ext_ref[index, 1 + j, SUB + rows :] = after[field, :, at]

    @pl.when(i == 0)
    def _():
        for j in range(count):
            at = slice(j * LANE, (j + 1) * LANE)
            ext_ref[index, 1 + j, SUB - RIM : SUB] = top_ref[index, :, at]

    @pl.when(i == n - 1)
    def _():
        for j in range(count):
            at = slice(j * LANE, (j + 1) * LANE)
            ext_ref[index, 1 + j, SUB + rows : SUB + rows + RIM] = low_ref[index, :, at]

    if left_ref.shape[1] == rows:
        ext_ref[index, 0, SUB : SUB + rows] = left_ref[index]
        ext_ref[index, 1 + count, SUB : SUB + rows] = right_ref[index]
    else:
        at = pl.ds(pl.multiple_of(i * rows, SUB), rows + 2 * SUB)
        ext_ref[index, 0] = left_ref[index, at]
        ext_ref[index, 1 + count] = right_ref[index, at]


def neighbours(x):
    count = x.shape[0] - 2
    lane = lax.broadcasted_iota(jnp.int32, (count, SUB, LANE), 2)
    out = []
    for by in (-2, -1):
        moved = pltpu.roll(x, -by, 2)
        out.append(jnp.where(lane < -by, moved[:count], moved[1 : 1 + count]))
    for by in (1, 2):
        moved = pltpu.roll(x, LANE - by, 2)
        out.append(jnp.where(lane >= LANE - by, moved[2:], moved[1 : 1 + count]))
    return out


def tile_count(count, most):
    while count % most:
        most -= 1
    return most


def spread(start, rows):
    if rows == SUB:
        return pl.ds(start, SUB)
    return pl.ds(start, SUB, stride=rows // SUB)


def vorticity_kernel(base_ref, *refs):
    planes, heights, dipoles, edge = refs[0:3], refs[3:6], refs[6:9], refs[9:13]
    o_ref, ext_ref = refs[13], refs[14]
    _, count, rows, _ = o_ref.shape
    i = base_ref[0] + pl.program_id(0)
    for index, (source, field) in enumerate(
        [(planes, 0), (planes, 1), (heights, 0), (dipoles, 0)]
    ):
        fill(ext_ref, index, source, field, edge, i, base_ref[1])
    many = tile_count(count, MANY)

    def body(t, _):
        for c in range(0, count, many):
            ga, gb = [], []
            for index in range(4):

                def load(s, lo, hi):
                    return ext_ref[index, lo:hi, spread(SUB + t + s, rows)]

                ga.append(diff_one(*[load(s, c + 1, c + 1 + many) for s in (-2, -1, 1, 2)]))
                gb.append(diff_one(*neighbours(load(0, c, c + many + 2))))
            _, _, normal = normal_of(ga, gb)
            inverse = 12.0 * lax.rsqrt(dot3(normal, normal))
            o_ref[0, c : c + many, spread(t, rows)] = ga[3] * inverse
            o_ref[1, c : c + many, spread(t, rows)] = gb[3] * inverse
        return 0

    lax.fori_loop(0, rows // SUB, body, 0)


def geometry_kernel(*refs):
    planes, heights, edge = refs[0:3], refs[3:6], refs[6:10]
    unit_ref, base_ref, ext_ref, first_ref, second_ref = refs[10:15]
    count, rows, _ = base_ref.shape
    i, n = pl.program_id(0), pl.num_programs(0)
    for index, (source, field) in enumerate([(planes, 0), (planes, 1), (heights, 0)]):
        fill(ext_ref, index, source, field, edge, i, n)
    many = tile_count(count, MANY)

    def along(g, _):
        at = pl.ds(pl.multiple_of(g * SUB, SUB), SUB)
        for c in range(0, count, many):
            for index in range(3):
                flat = ext_ref[index, c : c + many + 2, at]
                m2, m1, p1, p2 = neighbours(flat)
                first_ref[index, c : c + many, at] = diff_one(m2, m1, p1, p2)
                second_ref[index, c : c + many, at] = diff_two(m2, m1, flat[1 : 1 + many], p1, p2)
        return 0

    lax.fori_loop(0, rows // SUB + 2, along, 0)

    def body(t, _):
        for c in range(0, count, many):
            ga, gb, caa, cbb, cab = [], [], [], [], []
            for index in range(3):
                steps = (-2, -1, 0, 1, 2)
                v = [
                    ext_ref[index, c + 1 : c + 1 + many, spread(SUB + t + s, rows)] for s in steps
                ]
                ga.append(diff_one(v[0], v[1], v[3], v[4]))
                caa.append(diff_two(*v))
                f = [first_ref[index, c : c + many, spread(SUB + t + s, rows)] for s in steps]
                gb.append(f[2])
                cab.append(diff_one(f[0], f[1], f[3], f[4]))
                cbb.append(second_ref[index, c : c + many, spread(SUB + t, rows)])
                if index == 2:
                    height = v[2]
            a, b, normal = normal_of(ga, gb)
            inverse = lax.rsqrt(dot3(normal, normal))
            top = (
                dot3(a, a) * dot3(cbb, normal)
                - (2.0 / 12.0) * dot3(a, b) * dot3(cab, normal)
                + dot3(b, b) * dot3(caa, normal)
            )
            curvature = (0.5 * 12.0) * top * (inverse * inverse * inverse)
            at = (slice(c, c + many), spread(t, rows))
            for axis in range(3):
                unit_ref[(axis,) + at] = normal[axis] * inverse
            base_ref[at] = 0.3 * curvature - 0.5 * height
        return 0

    lax.fori_loop(0, rows // SUB, body, 0)


def row_step(rows):
    step = 64
    while rows % step:
        step //= 2
    return step


def block_specs(count, step, rows, width):
    per, total = step // SUB, rows // SUB

    def at(i, base):
        return i + base[0][0] if base else i

    return [
        pl.BlockSpec((count, step, width), lambda i, *base: (0, at(i, base), 0)),
        pl.BlockSpec(
            (count, SUB, width),
            lambda i, *base: (0, jnp.maximum(at(i, base) * per - 1, 0), 0),
        ),
        pl.BlockSpec(
            (count, SUB, width),
            lambda i, *base: (0, jnp.minimum((at(i, base) + 1) * per, total - 1), 0),
        ),
    ]


def vorticity_stage(planes, height, dipole, edge, which, parts):
    _, rows, width = planes.shape
    count = width // LANE
    part = rows // parts
    step = row_step(part)
    rim = lambda: pl.BlockSpec((4, step, LANE), lambda i, base: (0, i + base[0], 0))
    first = jnp.stack([which * (part // step), rows // step]).astype(jnp.int32)
    return pl.pallas_call(
        vorticity_kernel,
        grid_spec=pltpu.PrefetchScalarGridSpec(
            num_scalar_prefetch=1,
            grid=(part // step,),
            in_specs=block_specs(2, step, rows, width)
            + block_specs(1, step, rows, width)
            + block_specs(1, step, rows, width)
            + [whole(edge[0]), whole(edge[1]), rim(), rim()],
            out_specs=pl.BlockSpec((2, count, step, LANE), lambda i, base: (0, 0, i, 0)),
            scratch_shapes=[pltpu.VMEM((4, count + 2, step + 2 * SUB, LANE), F32)],
        ),
        out_shape=jax.ShapeDtypeStruct((2, count, part, LANE), F32),
        compiler_params=params(),
        cost_estimate=pl.CostEstimate(
            flops=80 * part * width, bytes_accessed=6 * 4 * part * width, transcendentals=part * width
        ),
        name="vorticity_stage",
    )(first, *[planes] * 3, *[height[None]] * 3, *[dipole[None]] * 3, *edge)


def geometry_stage(planes, height, edge):
    _, rows, width = planes.shape
    count = width // LANE
    step = row_step(rows)
    return pl.pallas_call(
        geometry_kernel,
        grid=(rows // step,),
        in_specs=block_specs(2, step, rows, width)
        + block_specs(1, step, rows, width)
        + [whole(e) for e in edge],
        out_specs=[
            pl.BlockSpec((3, count, step, LANE), lambda i: (0, 0, i, 0)),
            pl.BlockSpec((count, step, LANE), lambda i: (0, i, 0)),
        ],
        out_shape=[
            jax.ShapeDtypeStruct((3, count, rows, LANE), F32),
            jax.ShapeDtypeStruct((count, rows, LANE), F32),
        ],
        scratch_shapes=[
            pltpu.VMEM((3, count + 2, step + 2 * SUB, LANE), F32),
            pltpu.VMEM((3, count, step + 2 * SUB, LANE), F32),
            pltpu.VMEM((3, count, step + 2 * SUB, LANE), F32),
        ],
        compiler_params=params(),
        cost_estimate=pl.CostEstimate(
            flops=200 * rows * width, bytes_accessed=7 * 4 * rows * width, transcendentals=rows * width
        ),
        name="geometry_stage",
    )(*[planes] * 3, *[height[None]] * 3, *edge)


def final_kernel(base_ref, speed_ref, unit_ref, rest_ref, *refs):
    velocity_ref, update_ref = refs[-2:]
    for j in range(unit_ref.shape[1]):
        at = slice(j * LANE, (j + 1) * LANE)
        speed = speed_ref[j]
        for axis in range(3):
            velocity_ref[axis, :, at] = speed * unit_ref[axis, j]
        update_ref[:, at] = rest_ref[j] + 0.5 * speed * speed


def final_stage(speed, unit, rest, which, before):
    count, part, _ = speed.shape
    rows, width = unit.shape[2], count * LANE
    step = LANE if part % LANE == 0 else row_step(part)
    first = (which * (part // step))[None].astype(jnp.int32)
    n_before = len(before)
    return pl.pallas_call(
        final_kernel,
        grid_spec=pltpu.PrefetchScalarGridSpec(
            num_scalar_prefetch=1,
            grid=(part // step,),
            in_specs=[
                pl.BlockSpec((count, step, LANE), lambda i, base: (0, i, 0)),
                pl.BlockSpec((3, count, step, LANE), lambda i, base: (0, 0, i + base[0], 0)),
                pl.BlockSpec((count, step, LANE), lambda i, base: (0, i + base[0], 0)),
            ]
            + [pl.BlockSpec(memory_space=pl.ANY)] * n_before,
            out_specs=[
                pl.BlockSpec((3, step, width), lambda i, base: (0, i + base[0], 0)),
                pl.BlockSpec((step, width), lambda i, base: (i + base[0], 0)),
            ],
        ),
        out_shape=[
            jax.ShapeDtypeStruct((3, rows, width), F32),
            jax.ShapeDtypeStruct((rows, width), F32),
        ],
        input_output_aliases={4 + k: k for k in range(n_before)},
        compiler_params=params(),
        cost_estimate=pl.CostEstimate(
            flops=6 * part * width, bytes_accessed=9 * 4 * part * width, transcendentals=0
        ),
        name="final_stage",
    )(first, speed, unit, rest, *before)


def both_ways(last, initial, axis):
    devices = lax.axis_size(axis)
    up = [(i, (i + 1) % devices) for i in range(devices)]
    down = [(j, i) for i, j in up]
    return lax.ppermute(last, axis, up), lax.ppermute(initial, axis, down)


def local(shift_plane, height, dipole):
    _, rows, width = shift_plane.shape
    tr, tc = lax.axis_size("tr"), lax.axis_size("tc")
    devices = tr * tc
    row_count, col_count = rows * tr, width * tc
    part = rows // tc

    def cut(a, b, dim):
        pieces = [shift_plane, height[None], dipole[None]]
        return jnp.concatenate([lax.slice_in_dim(p, a, b, axis=dim) for p in pieces], 0)

    top, low = both_ways(cut(rows - RIM, rows, 1), cut(0, RIM, 1), "tr")
    left, right = both_ways(cut(width - LANE, width, 2), cut(0, LANE, 2), "tc")
    me = lax.axis_index("tc").astype(jnp.int32)
    edges = (top, low, left, right)
    pieces = []
    for away in range(1, tc):
        send = vorticity_stage(shift_plane, height, dipole, edges, (me + away) % tc, tc)
        pieces.append(lax.ppermute(send, "tc", [(i, (i + away) % tc) for i in range(tc)]))
    own = vorticity_stage(shift_plane, height, dipole, edges, me, tc)
    row_table, back_table = row_tables(col_count)
    spec = row_forward([own] + pieces, me, row_table)
    blocks = spec.shape[0]
    n = blocks * LANE // devices
    u = max(1, n // LANE)
    n = n // u
    pieces = LANE // n
    spec = spec.reshape(blocks, 4, pieces, n, part)
    spec = jnp.swapaxes(spec, 1, 2).reshape(devices, u, 4, n, part)
    columns = lax.all_to_all(spec, ("tr", "tc"), split_axis=0, concat_axis=0, tiled=True)

    ends = jnp.stack([top[:3], low[:3]])
    left_ends, right_ends = both_ways(ends[..., width - LANE :], ends[..., :LANE], "tc")
    spare = ((0, 0), (SUB - RIM, SUB - RIM), (0, 0))
    edge = (
        top[:3],
        low[:3],
        jnp.pad(jnp.concatenate([left_ends[0], left[:3], left_ends[1]], 1), spare),
        jnp.pad(jnp.concatenate([right_ends[0], right[:3], right_ends[1]], 1), spare),
    )
    unit, base = geometry_stage(shift_plane, height, edge)

    columns, unit, base = lax.optimization_barrier((columns, unit, base))
    direct = part % LANE == 0
    if not direct:
        columns = columns.transpose(1, 2, 3, 0, 4).reshape(1, u, 4, n, row_count)
    number = row_numbers(col_count).reshape(-1)
    signed = np.where(number >= col_count // 2, number - col_count, number)
    freq = (signed / col_count).astype(np.float32)
    freq = np.ascontiguousarray(np.broadcast_to(freq[:, None], (freq.size, LANE)))
    place = lax.axis_index(("tr", "tc")) * (u * n)
    mine = lax.dynamic_slice_in_dim(jnp.asarray(freq), place, u * n, 0).reshape(u, n, LANE)
    tables = col_tables(row_count, 1.0 / (row_count * col_count))
    partial = col_stage(columns, mine, tables)
    if not direct:
        partial = partial.reshape(u, 2, n, devices, part).transpose(3, 0, 1, 2, 4)
    back = lax.all_to_all(partial, ("tr", "tc"), split_axis=0, concat_axis=0, tiled=True)
    back = back.reshape(blocks, pieces, 2, n, part)
    back = jnp.swapaxes(back, 1, 2).reshape(blocks, 2, LANE, part)
    speeds = row_back(back, me, back_table, tc)
    outs = final_stage(speeds[0], unit, base, me, ())
    for away in range(1, tc):
        turn = [(i, (i + away) % tc) for i in range(tc)]
        speed = lax.ppermute(speeds[away], "tc", turn)
        outs = final_stage(speed, unit, base, (me - away) % tc, outs)
    return tuple(outs)


def solution(mesh):
    in_specs = (
        P(None, ("groups", "tr"), "tc"),
        P(("groups", "tr"), "tc"),
        P(("groups", "tr"), "tc"),
    )
    out_specs = (P(None, ("groups", "tr"), "tc"), P(("groups", "tr"), "tc"))
    return jax.shard_map(local, mesh=mesh, in_specs=in_specs, out_specs=out_specs, check_vma=False)
```

```python
import functools

import jax
import jax.numpy as jnp
import numpy as np
from jax import lax
from jax.experimental import pallas as pl
from jax.experimental.pallas import tpu as pltpu
from jax.sharding import PartitionSpec as P

LANE = 128
SUB = 8
MANY = 4
RIM = 2
CUTS = 2
SOME = 8
F32 = jnp.float32
BF16 = jnp.bfloat16
VMEM_LIMIT = 60 * 1024 * 1024


def times_unit(value, turn, count):
    re, im = value
    turn %= count
    if turn == 0:
        return value
    if 4 * turn == count:
        return (-im, re)
    if 2 * turn == count:
        return (-re, -im)
    if 4 * turn == 3 * count:
        return (im, -re)
    c = float(np.cos(2 * np.pi * turn / count))
    s = float(np.sin(2 * np.pi * turn / count))
    if 8 * turn % count == 0:
        h = abs(c)
        if c * s > 0:
            out = (h * (re - im), h * (re + im))
        else:
            out = (h * (re + im), h * (im - re))
        if c < 0:
            out = (-out[0], -out[1])
        return out
    return (c * re - s * im, c * im + s * re)


def add(p, q):
    return (p[0] + q[0], p[1] + q[1])


def sub(p, q):
    return (p[0] - q[0], p[1] - q[1])


def fft_list(vals, sign):
    n = len(vals)
    if n == 1:
        return vals
    if n == 2:
        return [add(vals[0], vals[1]), sub(vals[0], vals[1])]
    quarter = n // 4
    parts = [fft_list(vals[j::4], sign) for j in range(4)]
    out = [None] * n
    for k in range(quarter):
        t = [times_unit(parts[j][k], sign * j * k, n) for j in range(4)]
        a, b = add(t[0], t[2]), sub(t[0], t[2])
        c, d = add(t[1], t[3]), sub(t[1], t[3])
        d = (-d[1], d[0]) if sign > 0 else (d[1], -d[0])
        out[k] = add(a, c)
        out[k + quarter] = add(b, d)
        out[k + 2 * quarter] = sub(a, c)
        out[k + 3 * quarter] = sub(b, d)
    return out


def rfft_list(vals):
    n = len(vals)
    if n == 2:
        return [(vals[0] + vals[1], None), (vals[0] - vals[1], None)]
    even, odd = rfft_list(vals[0::2]), rfft_list(vals[1::2])
    out = [None] * (n // 2 + 1)
    out[0] = (even[0][0] + odd[0][0], None)
    out[n // 2] = (even[0][0] - odd[0][0], None)
    for k in range(1, n // 4):
        t = times_unit(odd[k], -k, n)
        out[k] = add(even[k], t)
        low = sub(even[k], t)
        out[n // 2 - k] = (low[0], -low[1])
    out[n // 4] = (even[n // 4][0], -odd[n // 4][0])
    return out


def irfft_list(spec):
    n = 2 * (len(spec) - 1)
    if n == 2:
        return [spec[0][0] + spec[1][0], spec[0][0] - spec[1][0]]
    q = n // 4
    even, odd = [None] * (q + 1), [None] * (q + 1)
    even[0] = (spec[0][0] + spec[n // 2][0], None)
    odd[0] = (spec[0][0] - spec[n // 2][0], None)
    for k in range(1, q):
        other = (spec[n // 2 - k][0], -spec[n // 2 - k][1])
        even[k] = add(spec[k], other)
        odd[k] = times_unit(sub(spec[k], other), k, n)
    even[q] = (2.0 * spec[q][0], None)
    odd[q] = (-2.0 * spec[q][1], None)
    out = [None] * n
    out[0::2] = irfft_list(even)
    out[1::2] = irfft_list(odd)
    return out


def hi_lo(table):
    hi = table.astype(np.float32).astype(jnp.bfloat16)
    lo = (table - hi.astype(np.float64)).astype(np.float32).astype(jnp.bfloat16)
    return hi, lo


def row_numbers(length):
    outer = length // LANE
    blocks, half = outer // 2, LANE // 2
    number = np.arange(blocks)[:, None] + outer * np.arange(LANE)[None, :]
    number[0, :half] = outer * np.arange(half)
    number[0, half:] = blocks + outer * np.arange(half)
    return number


def row_tables(length):
    outer = length // LANE
    blocks, half = outer // 2, LANE // 2
    number = row_numbers(length)
    place = np.arange(LANE)
    ahead = np.zeros((blocks, 2 * LANE, 2 * LANE))
    back = np.zeros((blocks, 2 * LANE, 2 * LANE))
    for k in range(blocks):
        theta = 2 * np.pi * ((number[k][:, None] * place[None, :]) % length) / length
        c, s = np.cos(theta), np.sin(theta)
        if k:
            ahead[k] = np.block([[c, s], [-s, c]])
            back[k] = np.block([[c.T, -s.T], [s.T, c.T]])
        else:
            zero = np.zeros((half, LANE))
            ahead[0] = np.block(
                [[c[:half], zero], [zero, c[half:]], [-s[:half], zero], [zero, -s[half:]]]
            )
            weight = np.full((half, 1), 2.0)
            weight[0] = 1.0
            back[0] = np.block(
                [
                    [(weight * c[:half]).T, zero.T, -(weight * s[:half]).T, zero.T],
                    [zero.T, 2 * c[half:].T, zero.T, -2 * s[half:].T],
                ]
            )
    def packed(t):
        return np.concatenate(hi_lo(t), axis=1)

    return packed(ahead), packed(back)


def col_tables(length, scale):
    outer = length // LANE
    place = np.arange(LANE)
    theta = 2 * np.pi * ((place[:, None] * place[None, :]) % LANE) / LANE
    c, s = np.cos(theta), np.sin(theta)
    ahead = np.block([[c, -s], [s, c]])
    turned = np.block([[s, -c], [c, s]])
    back = turned * scale
    def packed(t):
        hi, lo = hi_lo(t)
        return np.concatenate([hi, lo, hi], axis=0)

    first = np.arange(outer)[:, None]
    angle = 2 * np.pi * ((first * place[None, :]) % length) / length
    twist = np.stack([np.cos(angle), np.sin(angle)]).astype(np.float32)
    twist = np.ascontiguousarray(np.broadcast_to(twist[:, :, None, :], (2, outer, SUB, LANE)))
    number = first + outer * place[None, :]
    signed = np.where(number >= length // 2, number - length, number)
    freq = (signed / length).astype(np.float32)
    live = np.where(number == length // 2, 0.0, 0.5).astype(np.float32)
    freq = np.stack([freq, live])[:, :, None, :]
    freq = np.ascontiguousarray(np.broadcast_to(freq, (2, outer, SUB, LANE)))
    return packed(ahead), packed(back), twist, freq


def split(x):
    hi = x.astype(BF16)
    return hi, (x - hi.astype(F32)).astype(BF16)


def params(**more):
    return pltpu.CompilerParams(vmem_limit_bytes=VMEM_LIMIT, **more)


def whole(array):
    zeros = (0,) * array.ndim
    return pl.BlockSpec(array.shape, lambda *_: zeros, pipeline_mode=pl.Buffered(1))


def row_kernel(me_ref, *refs):
    x_refs, (w_ref, o_ref, s_ref) = refs[:-3], refs[-3:]
    sides = len(x_refs)
    first = pl.program_id(1) == 0
    for me in range(sides):

        @pl.when(jnp.logical_and(first, me_ref[0] == me))
        def _(me=me):
            row_short([x_refs[(me - side) % sides] for side in range(sides)], s_ref)

    row_long(w_ref, o_ref, s_ref, x_refs[0].shape[2])


def row_short(x_refs, s_ref):
    _, per, rows, _ = x_refs[0].shape
    outer = len(x_refs) * per
    blocks = outer // 2

    for field in range(2):

        def short(g, _, field=field):
            at = pl.ds(pl.multiple_of(g * SUB, SUB), SUB)
            vals = [x_refs[a // per][field, a % per, at] for a in range(outer)]
            spec = rfft_list(vals)
            to = pl.ds(pl.multiple_of(field * rows + g * SUB, SUB), SUB)
            s_ref[0, to, :LANE] = spec[0][0]
            s_ref[0, to, LANE:] = spec[blocks][0]
            for k in range(1, blocks):
                s_ref[k, to, :LANE] = spec[k][0]
                s_ref[k, to, LANE:] = spec[k][1]
            return 0

        lax.fori_loop(0, rows // SUB, short, 0)


def three(w, x, dims):
    hi, lo = split(x)
    out = w.shape[0] // 2
    both = lax.dot_general(w, hi, dims, preferred_element_type=F32)
    rest = lax.dot_general(w[:out], lo, dims, preferred_element_type=F32)
    return both[:out] + (both[out:] + rest)


def row_long(w_ref, o_ref, s_ref, rows):
    some = o_ref.shape[0]
    start = pl.program_id(1) * some

    def long(k, _):
        y = three(w_ref[k], s_ref[start + k], (((1,), (1,)), ((), ())))
        for field in range(2):
            for part in range(2):
                o_ref[k, 2 * field + part] = y[
                    part * LANE : (part + 1) * LANE, field * rows : (field + 1) * rows
                ]
        return 0

    lax.fori_loop(0, some, long, 0, unroll=True)


def row_forward(pieces, me, table):
    _, per, rows, _ = pieces[0].shape
    blocks = len(pieces) * per // 2
    some = SOME if blocks % SOME == 0 else 1
    step = LANE if rows % LANE == 0 else rows
    return pl.pallas_call(
        row_kernel,
        grid_spec=pltpu.PrefetchScalarGridSpec(
            num_scalar_prefetch=1,
            grid=(rows // step, blocks // some),
            in_specs=[
                pl.BlockSpec((2, per, step, LANE), lambda i, k, _: (0, 0, i, 0)) for _ in pieces
            ]
            + [pl.BlockSpec((some,) + table.shape[1:], lambda i, k, _: (k, 0, 0))],
            out_specs=pl.BlockSpec((some, 4, LANE, step), lambda i, k, _: (k, 0, 0, i)),
            scratch_shapes=[pltpu.VMEM((blocks, 2 * step, 2 * LANE), F32)],
        ),
        out_shape=jax.ShapeDtypeStruct((blocks, 4, LANE, rows), F32),
        compiler_params=params(),
        name="row_forward",
    )(me[None], *pieces, table)


def col_kernel(*refs, chunk, cuts):
    x_refs = refs[:cuts]
    f2_ref, wf_ref, wb_ref, tw_ref, f1_ref = refs[cuts : cuts + 5]
    o_refs, (a_ref, z_ref) = refs[cuts + 5 : -2], refs[-2:]
    count, length = x_refs[0].shape[-2:]
    per = length // LANE

    def where(a):
        lanes = slice((a % per) * LANE, (a % per + 1) * LANE)
        return a // per % cuts, a // per // cuts, lanes

    outer = tw_ref.shape[1]

    for field in range(2):

        def short(g, _, field=field):
            at = pl.ds(pl.multiple_of(g * SUB, SUB), SUB)

            def part(a, which):
                cut, source, lanes = where(a)
                return x_refs[cut][source, 0, 2 * field + which, at, lanes]

            spec = fft_list([(part(a, 0), part(a, 1)) for a in range(outer)], -1)
            for k in range(outer):
                re, im = spec[k]
                if k:
                    c, s = tw_ref[0, k], tw_ref[1, k]
                    re, im = (re * c + im * s, im * c - re * s)
                a_ref[field, k, at, :LANE] = re
                a_ref[field, k, at, LANE:] = im
            return 0

        lax.fori_loop(0, count // SUB, short, 0)

    f2 = f2_ref[0]
    f2_square = jnp.maximum(f2 * f2, 1e-30)

    def long(j, _):
        at = pl.ds(j * chunk, chunk)

        def product(x, w_ref):
            hi, lo = split(x.reshape(chunk * count, 2 * LANE))
            return jnp.dot(
                jnp.concatenate([hi, hi, lo], axis=1), w_ref[...], preferred_element_type=F32
            ).reshape(chunk, count, 2 * LANE)

        y0 = product(a_ref[0, at], wf_ref)
        y1 = product(a_ref[1, at], wf_ref)
        f1 = f1_ref[0, at][:, :1]
        factor = f1_ref[1, at][:, :1] * lax.rsqrt(f1 * f1 + f2_square[None])
        m0, m1 = factor * f1, factor * f2[None]
        m0 = jnp.concatenate([m0, m0], axis=-1)
        m1 = jnp.concatenate([m1, m1], axis=-1)
        z_ref[at] = product(m0 * y0 + m1 * y1, wb_ref)
        return 0

    lax.fori_loop(0, outer // chunk, long, 0)

    def last(g, _):
        at = pl.ds(pl.multiple_of(g * SUB, SUB), SUB)
        vals = []
        for k in range(outer):
            re, im = z_ref[k, at, :LANE], z_ref[k, at, LANE:]
            if k:
                c, s = tw_ref[0, k], tw_ref[1, k]
                re, im = (re * c - im * s, im * c + re * s)
            vals.append((re, im))
        res = fft_list(vals, 1)
        for a in range(outer):
            cut, source, lanes = where(a)
            o_refs[cut][source, 0, 0, at, lanes] = res[a][0]
            o_refs[cut][source, 0, 1, at, lanes] = res[a][1]
        return 0

    lax.fori_loop(0, count // SUB, last, 0)


def col_stage(xs, f2, tables):
    sources, u, _, n, rows = xs[0].shape
    cuts = len(xs)
    outer = sources * cuts * rows // LANE
    step = n
    while step > 32 and step % 2 == 0:
        step //= 2
    chunk = max(1, min(outer, 1024 // step))
    block = lambda count: pl.BlockSpec(
        (sources, 1, count, step, rows), lambda i, j: (0, i, 0, j, 0)
    )
    return pl.pallas_call(
        functools.partial(col_kernel, chunk=chunk, cuts=cuts),
        grid=(u, n // step),
        in_specs=[block(4)] * cuts
        + [pl.BlockSpec((1, step, LANE), lambda i, j: (i, j, 0))]
        + [whole(t) for t in tables],
        out_specs=[block(2)] * cuts,
        out_shape=[jax.ShapeDtypeStruct((sources, u, 2, n, rows), F32)] * cuts,
        scratch_shapes=[
            pltpu.VMEM((2, outer, step, 2 * LANE), F32),
            pltpu.VMEM((outer, step, 2 * LANE), F32),
        ],
        compiler_params=params(),
        name="col_stage",
    )(*xs, f2, *tables)


def back_kernel(me_ref, x_ref, w_ref, *refs):
    o_refs, (z_ref, t_ref) = refs[:-2], refs[-2:]
    some, _, _, rows = x_ref.shape
    start = pl.program_id(1) * some

    def long(k, _):
        x = x_ref[k].reshape(2 * LANE, rows)
        z_ref[start + k] = three(w_ref[k], x, (((1,), (0,)), ((), ())))
        return 0

    lax.fori_loop(0, some, long, 0, unroll=True)

    @pl.when(pl.program_id(1) == pl.num_programs(1) - 1)
    def _():
        back_short(me_ref, o_refs, z_ref, t_ref)


def back_short(me_ref, o_refs, z_ref, t_ref):
    sides = len(o_refs)
    per = o_refs[0].shape[0]
    blocks = z_ref.shape[0]
    outer = 2 * blocks

    def short(g, _):
        at = pl.ds(pl.multiple_of(g * SUB, SUB), SUB)
        low = pl.ds(pl.multiple_of(LANE + g * SUB, SUB), SUB)
        spec = [(z_ref[0, at], None)]
        spec += [(z_ref[k, at], z_ref[k, low]) for k in range(1, blocks)]
        spec += [(z_ref[0, low], None)]
        res = irfft_list(spec)
        for a in range(outer):
            t_ref[a, at] = res[a]
        return 0

    lax.fori_loop(0, LANE // SUB, short, 0)

    for me in range(sides):

        @pl.when(me_ref[0] == me)
        def _(me=me):
            for a in range(outer):
                o_refs[(a // per - me) % sides][a % per] = t_ref[a].T


def row_back(x, me, table, sides):
    blocks, _, _, rows = x.shape
    per = 2 * blocks // sides
    some = SOME if blocks % SOME == 0 else 1
    step = LANE if rows % LANE == 0 else rows
    return pl.pallas_call(
        back_kernel,
        grid_spec=pltpu.PrefetchScalarGridSpec(
            num_scalar_prefetch=1,
            grid=(rows // step, blocks // some),
            in_specs=[
                pl.BlockSpec((some, 2, LANE, step), lambda i, k, _: (k, 0, 0, i)),
                pl.BlockSpec((some,) + table.shape[1:], lambda i, k, _: (k, 0, 0)),
            ],
            out_specs=[pl.BlockSpec((per, step, LANE), lambda i, k, _: (0, i, 0))] * sides,
            scratch_shapes=[
                pltpu.VMEM((blocks, 2 * LANE, step), F32),
                pltpu.VMEM((2 * blocks, LANE, step), F32),
            ],
        ),
        out_shape=[jax.ShapeDtypeStruct((per, rows, LANE), F32)] * sides,
        compiler_params=params(),
        name="row_back",
    )(me[None], x, table)


def diff_one(m2, m1, p1, p2):
    return 8.0 * (p1 - m1) - (p2 - m2)


def diff_two(m2, m1, zero, p1, p2):
    return 16.0 * (p1 + m1) - (p2 + m2) - 30.0 * zero


def normal_of(ga, gb):
    a = (12.0 + ga[0], ga[1], ga[2])
    b = (gb[0], 12.0 + gb[1], gb[2])
    normal = (
        a[1] * b[2] - a[2] * b[1],
        a[2] * b[0] - a[0] * b[2],
        a[0] * b[1] - a[1] * b[0],
    )
    return a, b, normal


def dot3(p, q):
    return p[0] * q[0] + p[1] * q[1] + p[2] * q[2]


def fill(ext_ref, index, refs, field, edge, i, n):
    block, prev, after = refs
    rows, width = block.shape[-2:]
    count = width // LANE
    top_ref, low_ref, left_ref, right_ref = edge
    for j in range(count):
        at = slice(j * LANE, (j + 1) * LANE)
        ext_ref[index, 1 + j, SUB : SUB + rows] = block[field, :, at]
        ext_ref[index, 1 + j, :SUB] = prev[field, :, at]
        ext_ref[index, 1 + j, SUB + rows :] = after[field, :, at]

    @pl.when(i == 0)
    def _():
        for j in range(count):
            at = slice(j * LANE, (j + 1) * LANE)
            ext_ref[index, 1 + j, SUB - RIM : SUB] = top_ref[index, :, at]

    @pl.when(i == n - 1)
    def _():
        for j in range(count):
            at = slice(j * LANE, (j + 1) * LANE)
            ext_ref[index, 1 + j, SUB + rows : SUB + rows + RIM] = low_ref[index, :, at]

    if left_ref.shape[1] == rows:
        ext_ref[index, 0, SUB : SUB + rows] = left_ref[index]
        ext_ref[index, 1 + count, SUB : SUB + rows] = right_ref[index]
    else:
        at = pl.ds(pl.multiple_of(i * rows, SUB), rows + 2 * SUB)
        ext_ref[index, 0] = left_ref[index, at]
        ext_ref[index, 1 + count] = right_ref[index, at]


def neighbours(x):
    count = x.shape[0] - 2
    lane = lax.broadcasted_iota(jnp.int32, (count, SUB, LANE), 2)
    out = []
    for by in (-2, -1):
        moved = pltpu.roll(x, -by, 2)
        out.append(jnp.where(lane < -by, moved[:count], moved[1 : 1 + count]))
    for by in (1, 2):
        moved = pltpu.roll(x, LANE - by, 2)
        out.append(jnp.where(lane >= LANE - by, moved[2:], moved[1 : 1 + count]))
    return out


def tile_count(count, most):
    while count % most:
        most -= 1
    return most


def spread(start, rows):
    if rows == SUB:
        return pl.ds(start, SUB)
    return pl.ds(start, SUB, stride=rows // SUB)


def vorticity_kernel(base_ref, *refs):
    planes, heights, dipoles, edge = refs[0:3], refs[3:6], refs[6:9], refs[9:13]
    o_ref, ext_ref = refs[13], refs[14]
    _, count, rows, _ = o_ref.shape
    i = base_ref[0] + pl.program_id(0)
    for index, (source, field) in enumerate(
        [(planes, 0), (planes, 1), (heights, 0), (dipoles, 0)]
    ):
        fill(ext_ref, index, source, field, edge, i, base_ref[1])
    many = tile_count(count, MANY)

    def body(t, _):
        for c in range(0, count, many):
            ga, gb = [], []
            for index in range(4):

                def load(s, lo, hi):
                    return ext_ref[index, lo:hi, spread(SUB + t + s, rows)]

                ga.append(diff_one(*[load(s, c + 1, c + 1 + many) for s in (-2, -1, 1, 2)]))
                gb.append(diff_one(*neighbours(load(0, c, c + many + 2))))
            _, _, normal = normal_of(ga, gb)
            inverse = 12.0 * lax.rsqrt(dot3(normal, normal))
            o_ref[0, c : c + many, spread(t, rows)] = ga[3] * inverse
            o_ref[1, c : c + many, spread(t, rows)] = gb[3] * inverse
        return 0

    lax.fori_loop(0, rows // SUB, body, 0)


def geometry_kernel(*refs):
    planes, heights, edge = refs[0:3], refs[3:6], refs[6:10]
    unit_ref, base_ref, ext_ref, first_ref, second_ref = refs[10:15]
    count, rows, _ = base_ref.shape
    i, n = pl.program_id(0), pl.num_programs(0)
    for index, (source, field) in enumerate([(planes, 0), (planes, 1), (heights, 0)]):
        fill(ext_ref, index, source, field, edge, i, n)
    many = tile_count(count, MANY)

    def along(g, _):
        at = pl.ds(pl.multiple_of(g * SUB, SUB), SUB)
        for c in range(0, count, many):
            for index in range(3):
                flat = ext_ref[index, c : c + many + 2, at]
                m2, m1, p1, p2 = neighbours(flat)
                first_ref[index, c : c + many, at] = diff_one(m2, m1, p1, p2)
                second_ref[index, c : c + many, at] = diff_two(m2, m1, flat[1 : 1 + many], p1, p2)
        return 0

    lax.fori_loop(0, rows // SUB + 2, along, 0)

    def body(t, _):
        for c in range(0, count, many):
            ga, gb, caa, cbb, cab = [], [], [], [], []
            for index in range(3):
                steps = (-2, -1, 0, 1, 2)
                v = [
                    ext_ref[index, c + 1 : c + 1 + many, spread(SUB + t + s, rows)] for s in steps
                ]
                ga.append(diff_one(v[0], v[1], v[3], v[4]))
                caa.append(diff_two(*v))
                f = [first_ref[index, c : c + many, spread(SUB + t + s, rows)] for s in steps]
                gb.append(f[2])
                cab.append(diff_one(f[0], f[1], f[3], f[4]))
                cbb.append(second_ref[index, c : c + many, spread(SUB + t, rows)])
                if index == 2:
                    height = v[2]
            a, b, normal = normal_of(ga, gb)
            inverse = lax.rsqrt(dot3(normal, normal))
            top = (
                dot3(a, a) * dot3(cbb, normal)
                - (2.0 / 12.0) * dot3(a, b) * dot3(cab, normal)
                + dot3(b, b) * dot3(caa, normal)
            )
            curvature = (0.5 * 12.0) * top * (inverse * inverse * inverse)
            at = (slice(c, c + many), spread(t, rows))
            for axis in range(3):
                unit_ref[(axis,) + at] = normal[axis] * inverse
            base_ref[at] = 0.3 * curvature - 0.5 * height
        return 0

    lax.fori_loop(0, rows // SUB, body, 0)


def row_step(rows):
    step = 64
    while rows % step:
        step //= 2
    return step


def block_specs(count, step, rows, width):
    per, total = step // SUB, rows // SUB

    def at(i, base):
        return i + base[0][0] if base else i

    return [
        pl.BlockSpec((count, step, width), lambda i, *base: (0, at(i, base), 0)),
        pl.BlockSpec(
            (count, SUB, width),
            lambda i, *base: (0, jnp.maximum(at(i, base) * per - 1, 0), 0),
        ),
        pl.BlockSpec(
            (count, SUB, width),
            lambda i, *base: (0, jnp.minimum((at(i, base) + 1) * per, total - 1), 0),
        ),
    ]


def vorticity_stage(planes, height, dipole, edge, which, parts):
    _, rows, width = planes.shape
    count = width // LANE
    part = rows // parts
    step = row_step(part)
    rim = lambda: pl.BlockSpec((4, step, LANE), lambda i, base: (0, i + base[0], 0))
    first = jnp.stack([which * (part // step), rows // step]).astype(jnp.int32)
    return pl.pallas_call(
        vorticity_kernel,
        grid_spec=pltpu.PrefetchScalarGridSpec(
            num_scalar_prefetch=1,
            grid=(part // step,),
            in_specs=block_specs(2, step, rows, width)
            + block_specs(1, step, rows, width)
            + block_specs(1, step, rows, width)
            + [whole(edge[0]), whole(edge[1]), rim(), rim()],
            out_specs=pl.BlockSpec((2, count, step, LANE), lambda i, base: (0, 0, i, 0)),
            scratch_shapes=[pltpu.VMEM((4, count + 2, step + 2 * SUB, LANE), F32)],
        ),
        out_shape=jax.ShapeDtypeStruct((2, count, part, LANE), F32),
        compiler_params=params(),
        cost_estimate=pl.CostEstimate(
            flops=80 * part * width, bytes_accessed=6 * 4 * part * width, transcendentals=part * width
        ),
        name="vorticity_stage",
    )(first, *[planes] * 3, *[height[None]] * 3, *[dipole[None]] * 3, *edge)


def geometry_stage(planes, height, edge):
    _, rows, width = planes.shape
    count = width // LANE
    step = row_step(rows)
    return pl.pallas_call(
        geometry_kernel,
        grid=(rows // step,),
        in_specs=block_specs(2, step, rows, width)
        + block_specs(1, step, rows, width)
        + [whole(e) for e in edge],
        out_specs=[
            pl.BlockSpec((3, count, step, LANE), lambda i: (0, 0, i, 0)),
            pl.BlockSpec((count, step, LANE), lambda i: (0, i, 0)),
        ],
        out_shape=[
            jax.ShapeDtypeStruct((3, count, rows, LANE), F32),
            jax.ShapeDtypeStruct((count, rows, LANE), F32),
        ],
        scratch_shapes=[
            pltpu.VMEM((3, count + 2, step + 2 * SUB, LANE), F32),
            pltpu.VMEM((3, count, step + 2 * SUB, LANE), F32),
            pltpu.VMEM((3, count, step + 2 * SUB, LANE), F32),
        ],
        compiler_params=params(),
        cost_estimate=pl.CostEstimate(
            flops=200 * rows * width, bytes_accessed=7 * 4 * rows * width, transcendentals=rows * width
        ),
        name="geometry_stage",
    )(*[planes] * 3, *[height[None]] * 3, *edge)


def final_kernel(base_ref, speed_ref, unit_ref, rest_ref, *refs):
    velocity_ref, update_ref = refs[-2:]
    for j in range(unit_ref.shape[1]):
        at = slice(j * LANE, (j + 1) * LANE)
        speed = speed_ref[j]
        for axis in range(3):
            velocity_ref[axis, :, at] = speed * unit_ref[axis, j]
        update_ref[:, at] = rest_ref[j] + 0.5 * speed * speed


def final_stage(speed, unit, rest, which, before):
    count, part, _ = speed.shape
    rows, width = unit.shape[2], count * LANE
    step = row_step(part)
    first = (which * (part // step))[None].astype(jnp.int32)
    n_before = len(before)
    return pl.pallas_call(
        final_kernel,
        grid_spec=pltpu.PrefetchScalarGridSpec(
            num_scalar_prefetch=1,
            grid=(part // step,),
            in_specs=[
                pl.BlockSpec((count, step, LANE), lambda i, base: (0, i, 0)),
                pl.BlockSpec((3, count, step, LANE), lambda i, base: (0, 0, i + base[0], 0)),
                pl.BlockSpec((count, step, LANE), lambda i, base: (0, i + base[0], 0)),
            ]
            + [pl.BlockSpec(memory_space=pl.ANY)] * n_before,
            out_specs=[
                pl.BlockSpec((3, step, width), lambda i, base: (0, i + base[0], 0)),
                pl.BlockSpec((step, width), lambda i, base: (i + base[0], 0)),
            ],
        ),
        out_shape=[
            jax.ShapeDtypeStruct((3, rows, width), F32),
            jax.ShapeDtypeStruct((rows, width), F32),
        ],
        input_output_aliases={4 + k: k for k in range(n_before)},
        compiler_params=params(),
        cost_estimate=pl.CostEstimate(
            flops=6 * part * width, bytes_accessed=9 * 4 * part * width, transcendentals=0
        ),
        name="final_stage",
    )(first, speed, unit, rest, *before)


def both_ways(last, initial, axis):
    devices = lax.axis_size(axis)
    up = [(i, (i + 1) % devices) for i in range(devices)]
    down = [(j, i) for i, j in up]
    return lax.ppermute(last, axis, up), lax.ppermute(initial, axis, down)


def local(shift_plane, height, dipole):
    _, rows, width = shift_plane.shape
    tr, tc = lax.axis_size("tr"), lax.axis_size("tc")
    devices = tr * tc
    row_count, col_count = rows * tr, width * tc
    part = rows // tc

    def cut(a, b, dim):
        pieces = [shift_plane, height[None], dipole[None]]
        return jnp.concatenate([lax.slice_in_dim(p, a, b, axis=dim) for p in pieces], 0)

    top, low = both_ways(cut(rows - RIM, rows, 1), cut(0, RIM, 1), "tr")
    left, right = both_ways(cut(width - LANE, width, 2), cut(0, LANE, 2), "tc")
    me = lax.axis_index("tc").astype(jnp.int32)
    edges = (top, low, left, right)
    row_table, back_table = row_tables(col_count)
    direct = part % LANE == 0
    cuts = CUTS if part % (CUTS * LANE) == 0 else 1
    cut_rows = part // cuts
    blocks = col_count // LANE // 2
    n = blocks * LANE // devices
    u = max(1, n // LANE)
    n = n // u
    pieces = LANE // n

    def turn(x, away):
        return lax.ppermute(x, "tc", [(i, (i + away) % tc) for i in range(tc)])

    def swap(x):
        return lax.all_to_all(x, ("tr", "tc"), split_axis=0, concat_axis=0, tiled=True)

    columns = []
    for h in range(cuts):

        def stage(core):
            return vorticity_stage(
                shift_plane, height, dipole, edges, core * cuts + h, tc * cuts
            )

        sent = [turn(stage((me + away) % tc), away) for away in range(1, tc)]
        spec = row_forward([stage(me)] + sent, me, row_table)
        spec = spec.reshape(blocks, 4, pieces, n, cut_rows)
        spec = jnp.swapaxes(spec, 1, 2).reshape(devices, u, 4, n, cut_rows)
        if h + 1 < cuts:
            spec, edges = lax.optimization_barrier((spec, edges))
        columns.append(swap(spec))

    ends = jnp.stack([top[:3], low[:3]])
    left_ends, right_ends = both_ways(ends[..., width - LANE :], ends[..., :LANE], "tc")
    spare = ((0, 0), (SUB - RIM, SUB - RIM), (0, 0))
    edge = (
        top[:3],
        low[:3],
        jnp.pad(jnp.concatenate([left_ends[0], left[:3], left_ends[1]], 1), spare),
        jnp.pad(jnp.concatenate([right_ends[0], right[:3], right_ends[1]], 1), spare),
    )
    unit, base = geometry_stage(shift_plane, height, edge)

    columns, unit, base = lax.optimization_barrier((columns, unit, base))
    if not direct:
        columns = [columns[0].transpose(1, 2, 3, 0, 4).reshape(1, u, 4, n, row_count)]
    number = row_numbers(col_count).reshape(-1)
    signed = np.where(number >= col_count // 2, number - col_count, number)
    freq = (signed / col_count).astype(np.float32)
    freq = np.ascontiguousarray(np.broadcast_to(freq[:, None], (freq.size, LANE)))
    place = lax.axis_index(("tr", "tc")) * (u * n)
    mine = lax.dynamic_slice_in_dim(jnp.asarray(freq), place, u * n, 0).reshape(u, n, LANE)
    tables = col_tables(row_count, 1.0 / (row_count * col_count))
    partial = col_stage(columns, mine, tables)
    if not direct:
        partial = [partial[0].reshape(u, 2, n, devices, part).transpose(3, 0, 1, 2, 4)]
    backs = [swap(p) for p in partial]
    outs = ()
    for h in range(cuts):
        back, outs = lax.optimization_barrier((backs[h], outs))
        back = back.reshape(blocks, pieces, 2, n, cut_rows)
        back = jnp.swapaxes(back, 1, 2).reshape(blocks, 2, LANE, cut_rows)
        speeds = row_back(back, me, back_table, tc)
        outs = final_stage(speeds[0], unit, base, me * cuts + h, outs)
        for away in range(1, tc):
            speed = turn(speeds[away], away)
            outs = final_stage(speed, unit, base, (me - away) % tc * cuts + h, outs)
    return tuple(outs)


def solution(mesh):
    in_specs = (
        P(None, ("groups", "tr"), "tc"),
        P(("groups", "tr"), "tc"),
        P(("groups", "tr"), "tc"),
    )
    out_specs = (P(None, ("groups", "tr"), "tc"), P(("groups", "tr"), "tc"))
    return jax.shard_map(local, mesh=mesh, in_specs=in_specs, out_specs=out_specs, check_vma=False)
```

```python
import functools

import jax
import jax.numpy as jnp
import numpy as np
from jax import lax
from jax.experimental import pallas as pl
from jax.experimental.pallas import tpu as pltpu
from jax.sharding import PartitionSpec as P

LANE = 128
SUB = 8
MANY = 4
RIM = 2
CUTS = 2
SOME = 8
F32 = jnp.float32
BF16 = jnp.bfloat16
VMEM_LIMIT = 60 * 1024 * 1024


def times_unit(value, turn, count):
    re, im = value
    turn %= count
    if turn == 0:
        return value
    if 4 * turn == count:
        return (-im, re)
    if 2 * turn == count:
        return (-re, -im)
    if 4 * turn == 3 * count:
        return (im, -re)
    c = float(np.cos(2 * np.pi * turn / count))
    s = float(np.sin(2 * np.pi * turn / count))
    if 8 * turn % count == 0:
        h = abs(c)
        if c * s > 0:
            out = (h * (re - im), h * (re + im))
        else:
            out = (h * (re + im), h * (im - re))
        if c < 0:
            out = (-out[0], -out[1])
        return out
    return (c * re - s * im, c * im + s * re)


def add(p, q):
    return (p[0] + q[0], p[1] + q[1])


def sub(p, q):
    return (p[0] - q[0], p[1] - q[1])


def fft_list(vals, sign):
    n = len(vals)
    if n == 1:
        return vals
    if n == 2:
        return [add(vals[0], vals[1]), sub(vals[0], vals[1])]
    quarter = n // 4
    parts = [fft_list(vals[j::4], sign) for j in range(4)]
    out = [None] * n
    for k in range(quarter):
        t = [times_unit(parts[j][k], sign * j * k, n) for j in range(4)]
        a, b = add(t[0], t[2]), sub(t[0], t[2])
        c, d = add(t[1], t[3]), sub(t[1], t[3])
        d = (-d[1], d[0]) if sign > 0 else (d[1], -d[0])
        out[k] = add(a, c)
        out[k + quarter] = add(b, d)
        out[k + 2 * quarter] = sub(a, c)
        out[k + 3 * quarter] = sub(b, d)
    return out


def rfft_list(vals):
    n = len(vals)
    if n == 2:
        return [(vals[0] + vals[1], None), (vals[0] - vals[1], None)]
    even, odd = rfft_list(vals[0::2]), rfft_list(vals[1::2])
    out = [None] * (n // 2 + 1)
    out[0] = (even[0][0] + odd[0][0], None)
    out[n // 2] = (even[0][0] - odd[0][0], None)
    for k in range(1, n // 4):
        t = times_unit(odd[k], -k, n)
        out[k] = add(even[k], t)
        low = sub(even[k], t)
        out[n // 2 - k] = (low[0], -low[1])
    out[n // 4] = (even[n // 4][0], -odd[n // 4][0])
    return out


def irfft_list(spec):
    n = 2 * (len(spec) - 1)
    if n == 2:
        return [spec[0][0] + spec[1][0], spec[0][0] - spec[1][0]]
    q = n // 4
    even, odd = [None] * (q + 1), [None] * (q + 1)
    even[0] = (spec[0][0] + spec[n // 2][0], None)
    odd[0] = (spec[0][0] - spec[n // 2][0], None)
    for k in range(1, q):
        other = (spec[n // 2 - k][0], -spec[n // 2 - k][1])
        even[k] = add(spec[k], other)
        odd[k] = times_unit(sub(spec[k], other), k, n)
    even[q] = (2.0 * spec[q][0], None)
    odd[q] = (-2.0 * spec[q][1], None)
    out = [None] * n
    out[0::2] = irfft_list(even)
    out[1::2] = irfft_list(odd)
    return out


def hi_lo(table):
    hi = table.astype(np.float32).astype(jnp.bfloat16)
    lo = (table - hi.astype(np.float64)).astype(np.float32).astype(jnp.bfloat16)
    return hi, lo


def row_numbers(length):
    outer = length // LANE
    blocks, half = outer // 2, LANE // 2
    number = np.arange(blocks)[:, None] + outer * np.arange(LANE)[None, :]
    number[0, :half] = outer * np.arange(half)
    number[0, half:] = blocks + outer * np.arange(half)
    return number


def row_tables(length):
    outer = length // LANE
    blocks, half = outer // 2, LANE // 2
    number = row_numbers(length)
    place = np.arange(LANE)
    ahead = np.zeros((blocks, 2 * LANE, 2 * LANE))
    back = np.zeros((blocks, 2 * LANE, 2 * LANE))
    for k in range(blocks):
        theta = 2 * np.pi * ((number[k][:, None] * place[None, :]) % length) / length
        c, s = np.cos(theta), np.sin(theta)
        if k:
            ahead[k] = np.block([[c, s], [-s, c]])
            back[k] = np.block([[c.T, -s.T], [s.T, c.T]])
        else:
            zero = np.zeros((half, LANE))
            ahead[0] = np.block(
                [[c[:half], zero], [zero, c[half:]], [-s[:half], zero], [zero, -s[half:]]]
            )
            weight = np.full((half, 1), 2.0)
            weight[0] = 1.0
            back[0] = np.block(
                [
                    [(weight * c[:half]).T, zero.T, -(weight * s[:half]).T, zero.T],
                    [zero.T, 2 * c[half:].T, zero.T, -2 * s[half:].T],
                ]
            )
    def packed(t):
        return np.concatenate(hi_lo(t), axis=1)

    return packed(ahead), packed(back)


def col_tables(length, scale):
    outer = length // LANE
    place = np.arange(LANE)
    theta = 2 * np.pi * ((place[:, None] * place[None, :]) % LANE) / LANE
    c, s = np.cos(theta), np.sin(theta)
    ahead = np.block([[c, -s], [s, c]])
    turned = np.block([[s, -c], [c, s]])
    back = turned * scale
    def packed(t):
        hi, lo = hi_lo(t)
        return np.concatenate([hi, lo, hi], axis=0)

    first = np.arange(outer)[:, None]
    angle = 2 * np.pi * ((first * place[None, :]) % length) / length
    twist = np.stack([np.cos(angle), np.sin(angle)]).astype(np.float32)
    twist = np.ascontiguousarray(np.broadcast_to(twist[:, :, None, :], (2, outer, SUB, LANE)))
    number = first + outer * place[None, :]
    signed = np.where(number >= length // 2, number - length, number)
    freq = (signed / length).astype(np.float32)
    live = np.where(number == length // 2, 0.0, 0.5).astype(np.float32)
    freq = np.stack([freq, live])[:, :, None, :]
    freq = np.ascontiguousarray(np.broadcast_to(freq, (2, outer, SUB, LANE)))
    return packed(ahead), packed(back), twist, freq


def split(x):
    hi = x.astype(BF16)
    return hi, (x - hi.astype(F32)).astype(BF16)


def params(**more):
    return pltpu.CompilerParams(vmem_limit_bytes=VMEM_LIMIT, **more)


def whole(array):
    zeros = (0,) * array.ndim
    return pl.BlockSpec(array.shape, lambda *_: zeros, pipeline_mode=pl.Buffered(1))


def row_kernel(me_ref, *refs):
    x_refs, (w_ref, o_ref, s_ref) = refs[:-3], refs[-3:]
    sides = len(x_refs)
    first = pl.program_id(1) == 0
    for me in range(sides):

        @pl.when(jnp.logical_and(first, me_ref[0] == me))
        def _(me=me):
            row_short([x_refs[(me - side) % sides] for side in range(sides)], s_ref)

    row_long(w_ref, o_ref, s_ref, x_refs[0].shape[2])


def row_short(x_refs, s_ref):
    _, per, rows, _ = x_refs[0].shape
    outer = len(x_refs) * per
    blocks = outer // 2

    for field in range(2):

        def short(g, _, field=field):
            at = pl.ds(pl.multiple_of(g * SUB, SUB), SUB)
            vals = [x_refs[a // per][field, a % per, at] for a in range(outer)]
            spec = rfft_list(vals)
            to = pl.ds(pl.multiple_of(field * rows + g * SUB, SUB), SUB)
            s_ref[0, to, :LANE] = spec[0][0]
            s_ref[0, to, LANE:] = spec[blocks][0]
            for k in range(1, blocks):
                s_ref[k, to, :LANE] = spec[k][0]
                s_ref[k, to, LANE:] = spec[k][1]
            return 0

        lax.fori_loop(0, rows // SUB, short, 0)


def three(w, x, dims):
    hi, lo = split(x)
    out = w.shape[0] // 2
    both = lax.dot_general(w, hi, dims, preferred_element_type=F32)
    rest = lax.dot_general(w[:out], lo, dims, preferred_element_type=F32)
    return both[:out] + (both[out:] + rest)


def row_long(w_ref, o_ref, s_ref, rows):
    some = o_ref.shape[0]
    start = pl.program_id(1) * some

    def long(k, _):
        y = three(w_ref[k], s_ref[start + k], (((1,), (1,)), ((), ())))
        for field in range(2):
            for part in range(2):
                o_ref[k, 2 * field + part] = y[
                    part * LANE : (part + 1) * LANE, field * rows : (field + 1) * rows
                ]
        return 0

    lax.fori_loop(0, some, long, 0, unroll=True)


def row_forward(pieces, me, table):
    _, per, rows, _ = pieces[0].shape
    blocks = len(pieces) * per // 2
    some = SOME if blocks % SOME == 0 else 1
    step = LANE if rows % LANE == 0 else rows
    return pl.pallas_call(
        row_kernel,
        grid_spec=pltpu.PrefetchScalarGridSpec(
            num_scalar_prefetch=1,
            grid=(rows // step, blocks // some),
            in_specs=[pl.BlockSpec((2, per, step, LANE), lambda i, k, _: (0, 0, i, 0))] * len(pieces)
            + [pl.BlockSpec((some,) + table.shape[1:], lambda i, k, _: (k, 0, 0))],
            out_specs=pl.BlockSpec((some, 4, LANE, step), lambda i, k, _: (k, 0, 0, i)),
            scratch_shapes=[pltpu.VMEM((blocks, 2 * step, 2 * LANE), F32)],
        ),
        out_shape=jax.ShapeDtypeStruct((blocks, 4, LANE, rows), F32),
        compiler_params=params(),
        name="row_forward",
    )(me[None], *pieces, table)


def col_kernel(*refs, chunk, cuts):
    x_refs = refs[:cuts]
    f2_ref, wf_ref, wb_ref, tw_ref, f1_ref = refs[cuts : cuts + 5]
    o_refs, (a_ref, z_ref) = refs[cuts + 5 : -2], refs[-2:]
    count, length = x_refs[0].shape[-2:]
    per = length // LANE

    def where(a):
        lanes = slice((a % per) * LANE, (a % per + 1) * LANE)
        return a // per % cuts, a // per // cuts, lanes

    outer = tw_ref.shape[1]

    for field in range(2):

        def short(g, _, field=field):
            at = pl.ds(pl.multiple_of(g * SUB, SUB), SUB)

            def part(a, which):
                cut, source, lanes = where(a)
                return x_refs[cut][source, 0, 2 * field + which, at, lanes]

            spec = fft_list([(part(a, 0), part(a, 1)) for a in range(outer)], -1)
            for k in range(outer):
                re, im = spec[k]
                if k:
                    c, s = tw_ref[0, k], tw_ref[1, k]
                    re, im = (re * c + im * s, im * c - re * s)
                a_ref[field, k, at, :LANE] = re
                a_ref[field, k, at, LANE:] = im
            return 0

        lax.fori_loop(0, count // SUB, short, 0)

    f2 = f2_ref[0]
    f2_square = jnp.maximum(f2 * f2, 1e-30)

    def long(j, _):
        at = pl.ds(j * chunk, chunk)

        def product(x, w_ref):
            hi, lo = split(x.reshape(chunk * count, 2 * LANE))
            return jnp.dot(
                jnp.concatenate([hi, hi, lo], axis=1), w_ref[...], preferred_element_type=F32
            ).reshape(chunk, count, 2 * LANE)

        y0 = product(a_ref[0, at], wf_ref)
        y1 = product(a_ref[1, at], wf_ref)
        f1 = f1_ref[0, at][:, :1]
        factor = f1_ref[1, at][:, :1] * lax.rsqrt(f1 * f1 + f2_square[None])
        m0, m1 = factor * f1, factor * f2[None]
        m0 = jnp.concatenate([m0, m0], axis=-1)
        m1 = jnp.concatenate([m1, m1], axis=-1)
        z_ref[at] = product(m0 * y0 + m1 * y1, wb_ref)
        return 0

    lax.fori_loop(0, outer // chunk, long, 0)

    def last(g, _):
        at = pl.ds(pl.multiple_of(g * SUB, SUB), SUB)
        vals = []
        for k in range(outer):
            re, im = z_ref[k, at, :LANE], z_ref[k, at, LANE:]
            if k:
                c, s = tw_ref[0, k], tw_ref[1, k]
                re, im = (re * c - im * s, im * c + re * s)
            vals.append((re, im))
        res = fft_list(vals, 1)
        for a in range(outer):
            cut, source, lanes = where(a)
            o_refs[cut][source, 0, 0, at, lanes] = res[a][0]
            o_refs[cut][source, 0, 1, at, lanes] = res[a][1]
        return 0

    lax.fori_loop(0, count // SUB, last, 0)


def col_stage(xs, f2, tables):
    sources, u, _, n, rows = xs[0].shape
    cuts = len(xs)
    outer = sources * cuts * rows // LANE
    step = n
    while step > 32 and step % 2 == 0:
        step //= 2
    chunk = max(1, min(outer, 1024 // step))
    block = lambda count: pl.BlockSpec(
        (sources, 1, count, step, rows), lambda i, j: (0, i, 0, j, 0)
    )
    return pl.pallas_call(
        functools.partial(col_kernel, chunk=chunk, cuts=cuts),
        grid=(u, n // step),
        in_specs=[block(4)] * cuts
        + [pl.BlockSpec((1, step, LANE), lambda i, j: (i, j, 0))]
        + [whole(t) for t in tables],
        out_specs=[block(2)] * cuts,
        out_shape=[jax.ShapeDtypeStruct((sources, u, 2, n, rows), F32)] * cuts,
        scratch_shapes=[
            pltpu.VMEM((2, outer, step, 2 * LANE), F32),
            pltpu.VMEM((outer, step, 2 * LANE), F32),
        ],
        compiler_params=params(),
        name="col_stage",
    )(*xs, f2, *tables)


def back_kernel(me_ref, x_ref, w_ref, *refs):
    o_refs, (z_ref, t_ref) = refs[:-2], refs[-2:]
    some, _, _, rows = x_ref.shape
    start = pl.program_id(1) * some

    def long(k, _):
        x = x_ref[k].reshape(2 * LANE, rows)
        z_ref[start + k] = three(w_ref[k], x, (((1,), (0,)), ((), ())))
        return 0

    lax.fori_loop(0, some, long, 0, unroll=True)

    @pl.when(pl.program_id(1) == pl.num_programs(1) - 1)
    def _():
        back_short(me_ref, o_refs, z_ref, t_ref)


def back_short(me_ref, o_refs, z_ref, t_ref):
    sides = len(o_refs)
    per = o_refs[0].shape[0]
    blocks = z_ref.shape[0]
    outer = 2 * blocks

    def short(g, _):
        at = pl.ds(pl.multiple_of(g * SUB, SUB), SUB)
        low = pl.ds(pl.multiple_of(LANE + g * SUB, SUB), SUB)
        spec = [(z_ref[0, at], None)]
        spec += [(z_ref[k, at], z_ref[k, low]) for k in range(1, blocks)]
        spec += [(z_ref[0, low], None)]
        res = irfft_list(spec)
        for a in range(outer):
            t_ref[a, at] = res[a]
        return 0

    lax.fori_loop(0, LANE // SUB, short, 0)

    for me in range(sides):

        @pl.when(me_ref[0] == me)
        def _(me=me):
            for a in range(outer):
                o_refs[(a // per - me) % sides][a % per] = t_ref[a].T


def row_back(x, me, table, sides):
    blocks, _, _, rows = x.shape
    per = 2 * blocks // sides
    some = SOME if blocks % SOME == 0 else 1
    step = LANE if rows % LANE == 0 else rows
    return pl.pallas_call(
        back_kernel,
        grid_spec=pltpu.PrefetchScalarGridSpec(
            num_scalar_prefetch=1,
            grid=(rows // step, blocks // some),
            in_specs=[
                pl.BlockSpec((some, 2, LANE, step), lambda i, k, _: (k, 0, 0, i)),
                pl.BlockSpec((some,) + table.shape[1:], lambda i, k, _: (k, 0, 0)),
            ],
            out_specs=[pl.BlockSpec((per, step, LANE), lambda i, k, _: (0, i, 0))] * sides,
            scratch_shapes=[
                pltpu.VMEM((blocks, 2 * LANE, step), F32),
                pltpu.VMEM((2 * blocks, LANE, step), F32),
            ],
        ),
        out_shape=[jax.ShapeDtypeStruct((per, rows, LANE), F32)] * sides,
        compiler_params=params(),
        name="row_back",
    )(me[None], x, table)


def diff_one(m2, m1, p1, p2):
    return 8.0 * (p1 - m1) - (p2 - m2)


def diff_two(m2, m1, zero, p1, p2):
    return 16.0 * (p1 + m1) - (p2 + m2) - 30.0 * zero


def normal_of(ga, gb):
    a = (12.0 + ga[0], ga[1], ga[2])
    b = (gb[0], 12.0 + gb[1], gb[2])
    normal = (
        a[1] * b[2] - a[2] * b[1],
        a[2] * b[0] - a[0] * b[2],
        a[0] * b[1] - a[1] * b[0],
    )
    return a, b, normal


def dot3(p, q):
    return p[0] * q[0] + p[1] * q[1] + p[2] * q[2]


def fill(ext_ref, index, refs, field, edge, i, n):
    block, prev, after = refs
    rows, width = block.shape[-2:]
    count = width // LANE
    top_ref, low_ref, left_ref, right_ref = edge
    for j in range(count):
        at = slice(j * LANE, (j + 1) * LANE)
        ext_ref[index, 1 + j, SUB : SUB + rows] = block[field, :, at]
        ext_ref[index, 1 + j, :SUB] = prev[field, :, at]
        ext_ref[index, 1 + j, SUB + rows :] = after[field, :, at]

    @pl.when(i == 0)
    def _():
        for j in range(count):
            at = slice(j * LANE, (j + 1) * LANE)
            ext_ref[index, 1 + j, SUB - RIM : SUB] = top_ref[index, :, at]

    @pl.when(i == n - 1)
    def _():
        for j in range(count):
            at = slice(j * LANE, (j + 1) * LANE)
            ext_ref[index, 1 + j, SUB + rows : SUB + rows + RIM] = low_ref[index, :, at]

    if left_ref.shape[1] == rows:
        ext_ref[index, 0, SUB : SUB + rows] = left_ref[index]
        ext_ref[index, 1 + count, SUB : SUB + rows] = right_ref[index]
    else:
        at = pl.ds(pl.multiple_of(i * rows, SUB), rows + 2 * SUB)
        ext_ref[index, 0] = left_ref[index, at]
        ext_ref[index, 1 + count] = right_ref[index, at]


def neighbours(x):
    count = x.shape[0] - 2
    lane = lax.broadcasted_iota(jnp.int32, (count, SUB, LANE), 2)
    out = []
    for by in (-2, -1):
        moved = pltpu.roll(x, -by, 2)
        out.append(jnp.where(lane < -by, moved[:count], moved[1 : 1 + count]))
    for by in (1, 2):
        moved = pltpu.roll(x, LANE - by, 2)
        out.append(jnp.where(lane >= LANE - by, moved[2:], moved[1 : 1 + count]))
    return out


def tile_count(count, most):
    while count % most:
        most -= 1
    return most


def spread(start, rows):
    if rows == SUB:
        return pl.ds(start, SUB)
    return pl.ds(start, SUB, stride=rows // SUB)


def vorticity_kernel(me_ref, *refs, start, total):
    planes, heights, dipoles, edge = refs[0:3], refs[3:6], refs[6:9], refs[9:13]
    o_ref, ext_ref = refs[13], refs[14]
    _, count, rows, _ = o_ref.shape
    i = start(me_ref) + pl.program_id(0)
    for index, (source, field) in enumerate(
        [(planes, 0), (planes, 1), (heights, 0), (dipoles, 0)]
    ):
        fill(ext_ref, index, source, field, edge, i, total)
    lane = lax.broadcasted_iota(jnp.int32, (SUB, LANE), 1)

    def body(t, _):
        rolled = {}

        def roll(index, c, by):
            key = (index, c, by)
            if key not in rolled:
                x = ext_ref[index, c, spread(SUB + t, rows)]
                rolled[key] = pltpu.roll(x, (-by) % LANE, 1)
            return rolled[key]

        def shift(index, c, by):
            if by < 0:
                return jnp.where(lane < -by, roll(index, c - 1, by), roll(index, c, by))
            return jnp.where(lane >= LANE - by, roll(index, c + 1, by), roll(index, c, by))

        for c in range(count):
            ga, gb = [], []
            for index in range(4):
                v = [ext_ref[index, c + 1, spread(SUB + t + s, rows)] for s in (-2, -1, 1, 2)]
                ga.append(diff_one(*v))
                gb.append(diff_one(*[shift(index, c + 1, s) for s in (-2, -1, 1, 2)]))
            _, _, normal = normal_of(ga, gb)
            inverse = 12.0 * lax.rsqrt(dot3(normal, normal))
            o_ref[0, c, spread(t, rows)] = ga[3] * inverse
            o_ref[1, c, spread(t, rows)] = gb[3] * inverse
        return 0

    lax.fori_loop(0, rows // SUB, body, 0)


def geometry_kernel(*refs):
    planes, heights, edge = refs[0:3], refs[3:6], refs[6:10]
    unit_ref, base_ref, ext_ref, first_ref, second_ref = refs[10:15]
    count, rows, _ = base_ref.shape
    i, n = pl.program_id(0), pl.num_programs(0)
    for index, (source, field) in enumerate([(planes, 0), (planes, 1), (heights, 0)]):
        fill(ext_ref, index, source, field, edge, i, n)
    many = tile_count(count, MANY)

    def along(g, _):
        at = pl.ds(pl.multiple_of(g * SUB, SUB), SUB)
        for c in range(0, count, many):
            for index in range(3):
                flat = ext_ref[index, c : c + many + 2, at]
                m2, m1, p1, p2 = neighbours(flat)
                first_ref[index, c : c + many, at] = diff_one(m2, m1, p1, p2)
                second_ref[index, c : c + many, at] = diff_two(m2, m1, flat[1 : 1 + many], p1, p2)
        return 0

    lax.fori_loop(0, rows // SUB + 2, along, 0)

    def body(t, _):
        for c in range(0, count, many):
            ga, gb, caa, cbb, cab = [], [], [], [], []
            for index in range(3):
                steps = (-2, -1, 0, 1, 2)
                v = [
                    ext_ref[index, c + 1 : c + 1 + many, spread(SUB + t + s, rows)] for s in steps
                ]
                ga.append(diff_one(v[0], v[1], v[3], v[4]))
                caa.append(diff_two(*v))
                f = [first_ref[index, c : c + many, spread(SUB + t + s, rows)] for s in steps]
                gb.append(f[2])
                cab.append(diff_one(f[0], f[1], f[3], f[4]))
                cbb.append(second_ref[index, c : c + many, spread(SUB + t, rows)])
                if index == 2:
                    height = v[2]
            a, b, normal = normal_of(ga, gb)
            inverse = lax.rsqrt(dot3(normal, normal))
            top = (
                dot3(a, a) * dot3(cbb, normal)
                - (2.0 / 12.0) * dot3(a, b) * dot3(cab, normal)
                + dot3(b, b) * dot3(caa, normal)
            )
            curvature = (0.5 * 12.0) * top * (inverse * inverse * inverse)
            at = (slice(c, c + many), spread(t, rows))
            for axis in range(3):
                unit_ref[(axis,) + at] = normal[axis] * inverse
            base_ref[at] = 0.3 * curvature - 0.5 * height
        return 0

    lax.fori_loop(0, rows // SUB, body, 0)


def row_step(rows, step=64):
    while rows % step:
        step //= 2
    return step


def block_specs(count, step, rows, width, start=None):
    per, total = step // SUB, rows // SUB

    def at(i, me):
        return i + start(*me) if start else i

    return [
        pl.BlockSpec((count, step, width), lambda i, *me: (0, at(i, me), 0)),
        pl.BlockSpec(
            (count, SUB, width),
            lambda i, *me: (0, jnp.maximum(at(i, me) * per - 1, 0), 0),
        ),
        pl.BlockSpec(
            (count, SUB, width),
            lambda i, *me: (0, jnp.minimum((at(i, me) + 1) * per, total - 1), 0),
        ),
    ]


def vorticity_stage(planes, height, dipole, edge, me, part_of, parts):
    _, rows, width = planes.shape
    count = width // LANE
    part = rows // parts
    step = row_step(part, 32)

    def at(me_ref):
        return part_of(me_ref[0]) * (part // step)

    rim = lambda: pl.BlockSpec((4, step, LANE), lambda i, me: (0, i + at(me), 0))
    return pl.pallas_call(
        functools.partial(vorticity_kernel, start=at, total=rows // step),
        grid_spec=pltpu.PrefetchScalarGridSpec(
            num_scalar_prefetch=1,
            grid=(part // step,),
            in_specs=block_specs(2, step, rows, width, at)
            + block_specs(1, step, rows, width, at)
            + block_specs(1, step, rows, width, at)
            + [whole(edge[0]), whole(edge[1]), rim(), rim()],
            out_specs=pl.BlockSpec((2, count, step, LANE), lambda i, me: (0, 0, i, 0)),
            scratch_shapes=[pltpu.VMEM((4, count + 2, step + 2 * SUB, LANE), F32)],
        ),
        out_shape=jax.ShapeDtypeStruct((2, count, part, LANE), F32),
        compiler_params=params(),
        cost_estimate=pl.CostEstimate(
            flops=80 * part * width, bytes_accessed=6 * 4 * part * width, transcendentals=part * width
        ),
        name="vorticity_stage",
    )(me[None], *[planes] * 3, *[height[None]] * 3, *[dipole[None]] * 3, *edge)


def geometry_stage(planes, height, edge):
    _, rows, width = planes.shape
    count = width // LANE
    step = row_step(rows)
    return pl.pallas_call(
        geometry_kernel,
        grid=(rows // step,),
        in_specs=block_specs(2, step, rows, width)
        + block_specs(1, step, rows, width)
        + [whole(e) for e in edge],
        out_specs=[
            pl.BlockSpec((3, count, step, LANE), lambda i: (0, 0, i, 0)),
            pl.BlockSpec((count, step, LANE), lambda i: (0, i, 0)),
        ],
        out_shape=[
            jax.ShapeDtypeStruct((3, count, rows, LANE), F32),
            jax.ShapeDtypeStruct((count, rows, LANE), F32),
        ],
        scratch_shapes=[
            pltpu.VMEM((3, count + 2, step + 2 * SUB, LANE), F32),
            pltpu.VMEM((3, count, step + 2 * SUB, LANE), F32),
            pltpu.VMEM((3, count, step + 2 * SUB, LANE), F32),
        ],
        compiler_params=params(),
        cost_estimate=pl.CostEstimate(
            flops=200 * rows * width, bytes_accessed=7 * 4 * rows * width, transcendentals=rows * width
        ),
        name="geometry_stage",
    )(*[planes] * 3, *[height[None]] * 3, *edge)


def final_kernel(me_ref, speed_ref, unit_ref, rest_ref, *refs):
    velocity_ref, update_ref = refs[-2:]
    for j in range(unit_ref.shape[1]):
        at = slice(j * LANE, (j + 1) * LANE)
        speed = speed_ref[j]
        for axis in range(3):
            velocity_ref[axis, :, at] = speed * unit_ref[axis, j]
        update_ref[:, at] = rest_ref[j] + 0.5 * speed * speed


def final_stage(speed, unit, rest, me, part_of, before):
    count, part, _ = speed.shape
    rows, width = unit.shape[2], count * LANE
    step = row_step(part)

    def at(me_ref):
        return part_of(me_ref[0]) * (part // step)

    n_before = len(before)
    return pl.pallas_call(
        final_kernel,
        grid_spec=pltpu.PrefetchScalarGridSpec(
            num_scalar_prefetch=1,
            grid=(part // step,),
            in_specs=[
                pl.BlockSpec((count, step, LANE), lambda i, me: (0, i, 0)),
                pl.BlockSpec((3, count, step, LANE), lambda i, me: (0, 0, i + at(me), 0)),
                pl.BlockSpec((count, step, LANE), lambda i, me: (0, i + at(me), 0)),
            ]
            + [pl.BlockSpec(memory_space=pl.ANY)] * n_before,
            out_specs=[
                pl.BlockSpec((3, step, width), lambda i, me: (0, i + at(me), 0)),
                pl.BlockSpec((step, width), lambda i, me: (i + at(me), 0)),
            ],
        ),
        out_shape=[
            jax.ShapeDtypeStruct((3, rows, width), F32),
            jax.ShapeDtypeStruct((rows, width), F32),
        ],
        input_output_aliases={4 + k: k for k in range(n_before)},
        compiler_params=params(),
        cost_estimate=pl.CostEstimate(
            flops=6 * part * width, bytes_accessed=9 * 4 * part * width, transcendentals=0
        ),
        name="final_stage",
    )(me[None], speed, unit, rest, *before)


def edge_kernel(*refs):
    ins, (last_ref, first_ref, low_ref, top_ref) = refs[:12], refs[12:]
    for k, field in enumerate((0, 1, 0, 0)):
        source = max(k - 1, 0) * 4
        last_ref[k] = ins[source][field]
        first_ref[k] = ins[source + 1][field]
        low_ref[k] = ins[source + 2][field, SUB - RIM :]
        top_ref[k] = ins[source + 3][field, :RIM]


def edge_stage(planes, height, dipole):
    _, rows, width = planes.shape
    specs, args = [], []
    for x in (planes, height[None], dipole[None]):
        c = x.shape[0]
        specs += [
            pl.BlockSpec((c, rows, LANE), lambda i: (0, 0, width // LANE - 1)),
            pl.BlockSpec((c, rows, LANE), lambda i: (0, 0, 0)),
            pl.BlockSpec((c, SUB, width), lambda i: (0, rows // SUB - 1, 0)),
            pl.BlockSpec((c, SUB, width), lambda i: (0, 0, 0)),
        ]
        args += [x] * 4
    strip = jax.ShapeDtypeStruct((4, rows, LANE), F32)
    rim = jax.ShapeDtypeStruct((4, RIM, width), F32)
    return pl.pallas_call(
        edge_kernel,
        grid=(1,),
        in_specs=specs,
        out_specs=[pl.BlockSpec(o.shape, lambda i: (0, 0, 0)) for o in (strip, strip, rim, rim)],
        out_shape=[strip, strip, rim, rim],
        compiler_params=params(),
        name="edge_stage",
    )(*args)


def both_ways(last, initial, axis):
    devices = lax.axis_size(axis)
    up = [(i, (i + 1) % devices) for i in range(devices)]
    down = [(j, i) for i, j in up]
    return lax.ppermute(last, axis, up), lax.ppermute(initial, axis, down)


def local(shift_plane, height, dipole):
    _, rows, width = shift_plane.shape
    tr, tc = lax.axis_size("tr"), lax.axis_size("tc")
    devices = tr * tc
    row_count, col_count = rows * tr, width * tc
    part = rows // tc

    last, initial, last_rows, initial_rows = edge_stage(shift_plane, height, dipole)
    top, low = both_ways(last_rows, initial_rows, "tr")
    left, right = both_ways(last, initial, "tc")
    me = lax.axis_index("tc").astype(jnp.int32)
    edges = (top, low, left, right)
    row_table, back_table = row_tables(col_count)
    direct = part % LANE == 0
    cuts = CUTS if part % (CUTS * LANE) == 0 else 1
    cut_rows = part // cuts
    blocks = col_count // LANE // 2
    n = blocks * LANE // devices
    u = max(1, n // LANE)
    n = n // u
    pieces = LANE // n

    def turn(x, away):
        return lax.ppermute(x, "tc", [(i, (i + away) % tc) for i in range(tc)])

    def swap(x):
        return lax.all_to_all(x, ("tr", "tc"), split_axis=0, concat_axis=0, tiled=True)

    columns = []
    for h in range(cuts):

        def stage(away):
            part_of = lambda core, h=h: lax.rem(core + away, tc) * cuts + h
            return vorticity_stage(shift_plane, height, dipole, edges, me, part_of, tc * cuts)

        sent = [turn(stage(away), away) for away in range(1, tc)]
        spec = row_forward([stage(0)] + sent, me, row_table)
        spec = spec.reshape(blocks, 4, pieces, n, cut_rows)
        spec = jnp.swapaxes(spec, 1, 2).reshape(devices, u, 4, n, cut_rows)
        if h + 1 < cuts:
            spec, edges = lax.optimization_barrier((spec, edges))
        columns.append(swap(spec))

    ends = jnp.stack([top[:3], low[:3]])
    left_ends, right_ends = both_ways(ends[..., width - LANE :], ends[..., :LANE], "tc")
    spare = ((0, 0), (SUB - RIM, SUB - RIM), (0, 0))
    edge = (
        top[:3],
        low[:3],
        jnp.pad(jnp.concatenate([left_ends[0], left[:3], left_ends[1]], 1), spare),
        jnp.pad(jnp.concatenate([right_ends[0], right[:3], right_ends[1]], 1), spare),
    )
    unit, base = geometry_stage(shift_plane, height, edge)

    columns, unit, base = lax.optimization_barrier((columns, unit, base))
    if not direct:
        columns = [columns[0].transpose(1, 2, 3, 0, 4).reshape(1, u, 4, n, row_count)]
    number = row_numbers(col_count).reshape(-1)
    signed = np.where(number >= col_count // 2, number - col_count, number)
    freq = (signed / col_count).astype(np.float32)
    freq = np.ascontiguousarray(np.broadcast_to(freq[:, None], (freq.size, LANE)))
    place = lax.axis_index(("tr", "tc")) * (u * n)
    mine = lax.dynamic_slice_in_dim(jnp.asarray(freq), place, u * n, 0).reshape(u, n, LANE)
    tables = col_tables(row_count, 1.0 / (row_count * col_count))
    partial = col_stage(columns, mine, tables)
    if not direct:
        partial = [partial[0].reshape(u, 2, n, devices, part).transpose(3, 0, 1, 2, 4)]
    backs = [swap(p) for p in partial]
    outs = ()
    for h in range(cuts):
        back, outs = lax.optimization_barrier((backs[h], outs))
        back = back.reshape(blocks, pieces, 2, n, cut_rows)
        back = jnp.swapaxes(back, 1, 2).reshape(blocks, 2, LANE, cut_rows)
        speeds = row_back(back, me, back_table, tc)
        for away in range(tc):
            speed = turn(speeds[away], away) if away else speeds[0]
            part_of = lambda core, h=h, away=away: lax.rem(core + tc - away, tc) * cuts + h
            outs = final_stage(speed, unit, base, me, part_of, outs)
    return tuple(outs)


def solution(mesh):
    in_specs = (
        P(None, ("groups", "tr"), "tc"),
        P(("groups", "tr"), "tc"),
        P(("groups", "tr"), "tc"),
    )
    out_specs = (P(None, ("groups", "tr"), "tc"), P(("groups", "tr"), "tc"))
    return jax.shard_map(local, mesh=mesh, in_specs=in_specs, out_specs=out_specs, check_vma=False)
```
